512 devices in a mesh: section: 32 (over z, x_lo), tensor: 16 (over x_hi, y, core).
Axes of the slice: x: 4 (x_hi: 2, x_lo: 2; x = x_hi * 2 + x_lo), y: 4, z: 16, core: 2. Of those that a mesh axis runs over, the one named last changes fastest.
Arguments:
- inputs: bfloat16 [32, 256, 2048], P('section', None, 'tensor'), may hold values from -6 to 6
- out_grads: bfloat16 [32, 256, 2048], P('section', None, 'tensor'), may hold values from -1.5 to 1.5
- parked_store: bfloat16 [32, 2, 256, 2048], P('section', None, None, 'tensor'), may hold values from -6 to 6
- fetch_slot: int32 [32], P('section'), may hold values from 0 to 1
- norm_gain: float32 [32, 2048], P('section'), may hold values from 0.5 to 1.5
- weight_in: bfloat16 [32, 2048, 4096], P('section', None, 'tensor'), may hold values from -0.125 to 0.125
- weight_out: bfloat16 [32, 4096, 2048], P('section', 'tensor'), may hold values from -0.09375 to 0.09375
Outputs:
- arrivals: bfloat16 [32, 256, 2048], P('section', None, 'tensor')
- sent_grads: bfloat16 [32, 256, 2048], P('section', None, 'tensor')
- parked: bfloat16 [32, 256, 2048], P('section', None, 'tensor')
- weight_in_grad: bfloat16 [32, 2048, 4096], P('section', None, 'tensor')
- weight_out_grad: bfloat16 [32, 4096, 2048], P('section', 'tensor')
The draws below stay inside these ranges and needn't reach their ends.
All inputs are finite; a program needn't handle non-finite values.
Results may differ from the reference program's by a relative error of at most 0.014.
Values may be sent and summed in bfloat16 or wider, within the bound.
No kernel may reach another device: no remote copies, remote signals or barrier semaphores. Data moves between devices by JAX's collectives and lax.ppermute only.
A program may use at most 64 MiB of HBM per device.

```python
import jax
import jax.numpy as jnp
from jax import lax

D = 2048
FF = 4096
MB = 256
SLOTS = 2
SECTIONS = 32
N_TENSOR = 16


def touch_ends(drawn, stream_key, low, largest):
    longest = drawn.shape.index(max(drawn.shape))
    spots = []
    for shift in (0, 1):
        where = [jax.random.randint(jax.random.fold_in(stream_key, axis), (), 0, length) for axis, length in enumerate(drawn.shape)]
        where[longest] = (where[longest] + shift) % drawn.shape[longest]
        spots.append(tuple(where))
    return drawn.at[spots[0]].set(low).at[spots[1]].set(largest)


def block_scale(rng, extent, cuts, low, top_value):
    level = 1.0
    for dim, shards_of in cuts:
        heights = jax.random.uniform(jax.random.fold_in(jax.random.fold_in(rng, 6), dim), (shards_of,), jnp.float32, low / len(cuts), top_value / len(cuts))
        level = level * jnp.repeat(jnp.exp(heights), extent[dim] // shards_of).reshape((-1,) + (1,) * (len(extent) - 1 - dim))
    return level


def bell_draw(rng, extent, width, most, cuts=(), held_as=jnp.bfloat16):
    level = block_scale(rng, extent, cuts, -0.22, 0.18) if cuts else 1.0
    drawn = jax.random.normal(rng, extent, jnp.float32) * width * level
    return jnp.minimum(jnp.maximum(drawn, -most), most).astype(held_as)


def setup_inputs(seed: int = 0) -> dict:
    keys = jax.random.split(jax.random.key(seed), 8)
    inputs = bell_draw(keys[0], (SECTIONS, MB, D), 1.0, 6.0, ((0, 32), (2, 16)))
    out_grads = bell_draw(keys[1], (SECTIONS, MB, D), 0.25, 1.5, ((0, 32), (2, 16)))
    parked_store = bell_draw(keys[2], (SECTIONS, SLOTS, MB, D), 1.0, 6.0, ((0, 32), (3, 16)))
    fetch_slot = touch_ends(jax.random.randint(keys[3], (SECTIONS,), 0, SLOTS), jax.random.fold_in(keys[3], 1), 0, SLOTS - 1).astype(jnp.int32)
    norm_gain = jnp.clip(1.0 + 0.1 * jax.random.normal(keys[4], (SECTIONS, D), jnp.float32), 0.5, 1.5)
    weight_in = bell_draw(keys[5], (SECTIONS, D, FF), D ** -0.5, 0.125, ((0, 32), (2, 16)))
    weight_out = bell_draw(keys[6], (SECTIONS, FF, D), FF ** -0.5, 0.09375, ((0, 32), (1, 16)))
    return {"inputs": inputs, "out_grads": out_grads, "parked_store": parked_store, "fetch_slot": fetch_slot, "norm_gain": norm_gain, "weight_in": weight_in, "weight_out": weight_out}


EPSILON = 1e-05
GELU_ROOT = 0.7978845608028654
GELU_CUBIC = 0.044715

def gelu_value(values):
    inner = GELU_ROOT * (values + GELU_CUBIC * values * values * values)
    return 0.5 * values * (1.0 + jnp.tanh(inner))

def gelu_slope(values):
    inner = GELU_ROOT * (values + GELU_CUBIC * values * values * values)
    tangent = jnp.tanh(inner)
    return 0.5 * (1.0 + tangent) + 0.5 * values * (1.0 - tangent * tangent) * GELU_ROOT * (1.0 + 3.0 * GELU_CUBIC * values * values)

def grouped_sum(left, right, form):
    terms = jnp.einsum(form, left.astype(jnp.float32), right.astype(jnp.float32))
    rounded = lax.optimization_barrier(terms.astype(jnp.bfloat16))
    return lax.optimization_barrier(jnp.sum(rounded.astype(jnp.float32), axis=0))

def normalize(values, gain_row):
    values_f = values.astype(jnp.float32)
    center = lax.optimization_barrier(jnp.mean(values_f, axis=1))
    second = lax.optimization_barrier(jnp.mean(values_f * values_f, axis=1))
    scale = lax.rsqrt(second - center * center + EPSILON)
    hidden = (values_f - center[:, None]) * scale[:, None]
    normed = (hidden * gain_row[None, :]).astype(jnp.bfloat16)
    return (values_f, scale, hidden, normed)

def section_pass(items):
    forward_in, grad_out, fetched, gain_row, weight_a, weight_b = items
    inner = FF // N_TENSOR
    forward_f, scale, hidden_fwd, normed = normalize(forward_in, gain_row)
    pre = jnp.dot(normed, weight_a, preferred_element_type=jnp.float32)
    act = gelu_value(pre).astype(jnp.bfloat16)
    branch = grouped_sum(act.reshape(MB, N_TENSOR, inner), weight_b.reshape(N_TENSOR, inner, D), 'mjr,jrd->jmd')
    outputs = (forward_f + branch).astype(jnp.bfloat16)
    back_f, back_scale, hidden, back_normed = normalize(fetched, gain_row)
    back_pre = jnp.dot(back_normed, weight_a, preferred_element_type=jnp.float32)
    back_act = gelu_value(back_pre).astype(jnp.bfloat16)
    act_grad = jnp.dot(grad_out, weight_b.T, preferred_element_type=jnp.float32)
    pre_grad = (act_grad * gelu_slope(back_pre)).astype(jnp.bfloat16)
    normed_grad = grouped_sum(pre_grad.reshape(MB, N_TENSOR, inner), weight_a.reshape(D, N_TENSOR, inner), 'mjr,djr->jmd')
    scaled_grad = normed_grad * gain_row[None, :]
    plain_mean = lax.optimization_barrier(jnp.sum(scaled_grad, axis=1)) / D
    moment_mean = lax.optimization_barrier(jnp.sum(scaled_grad * hidden, axis=1)) / D
    input_grad = (grad_out.astype(jnp.float32) + back_scale[:, None] * (scaled_grad - plain_mean[:, None] - hidden * moment_mean[:, None])).astype(jnp.bfloat16)
    grad_a = jnp.dot(back_normed.T, pre_grad, preferred_element_type=jnp.float32).astype(jnp.bfloat16)
    grad_b = jnp.dot(back_act.T, grad_out, preferred_element_type=jnp.float32).astype(jnp.bfloat16)
    return (outputs, input_grad, grad_a, grad_b)

def reference(inputs, out_grads, parked_store, fetch_slot, norm_gain, weight_in, weight_out):
    section_count = inputs.shape[0]
    returned = parked_store[jnp.arange(section_count).astype(jnp.int32), fetch_slot.astype(jnp.int32)]
    fetched = returned[::-1]
    parked = inputs[::-1]
    outputs, input_grad, grad_a, grad_b = lax.map(section_pass, (inputs, out_grads, fetched, norm_gain, weight_in, weight_out))
    blank = jnp.zeros_like(outputs[:1])
    arrivals = jnp.concatenate([blank, outputs[:-1]], axis=0)
    sent_grads = jnp.concatenate([input_grad[1:], blank], axis=0)
    return (arrivals, sent_grads, parked, grad_a, grad_b)
```

```python
import functools

import jax
import jax.numpy as jnp
from jax import lax
from jax.experimental import pallas as pl
from jax.experimental.pallas import tpu as pltpu
from jax.sharding import PartitionSpec as P

EPSILON = 1e-05
GELU_ROOT = 0.7978845608028654
GELU_CUBIC = 0.044715

BF = jnp.bfloat16
F32 = jnp.float32
ROWS = 16
VMEM_LIMIT = 48 * 2**20


def vmem(count):
    return [pl.BlockSpec(memory_space=pltpu.VMEM)] * count


def dot(left, right, dims=((1,), (0,))):
    return lax.dot_general(left, right, (dims, ((), ())), preferred_element_type=F32)


def gelu_parts(values):
    inner = GELU_ROOT * (values + GELU_CUBIC * values * values * values)
    return jnp.tanh(inner)


def split_two(values):
    high = values.astype(BF)
    low = (values - high.astype(F32)).astype(BF)
    return high, low


def sums_to_rows(first, second):
    tokens = first.shape[0]
    parts = [part.astype(F32) for value in (first, second) for part in split_two(value)]
    lane = lax.broadcasted_iota(jnp.int32, (tokens, 128), 1)
    wide = jnp.zeros((tokens, 128), F32)
    for index, part in enumerate(parts):
        wide = jnp.where(lane == index, part, wide)
    tall = wide.T
    return jnp.concatenate([tall[:8, :128], tall[:8, 128:]], axis=0).astype(BF)


def resplit(rows_f):
    out = []
    for half in (0, 8):
        for stat in (0, 2):
            total = rows_f[half + stat : half + stat + 1] + rows_f[half + stat + 1 : half + stat + 2]
            out += list(split_two(total))
        out.append(jnp.zeros((4, rows_f.shape[1]), BF))
    return jnp.concatenate([part.astype(F32) for part in out], axis=0).astype(BF)


def both_cores(me, near, far):
    return jnp.concatenate([jnp.where(me == 0, near, far), jnp.where(me == 0, far, near)], axis=1)


def block_kernel(core, near, far, gain, weight_a, weight_b, own, other, normed_out, pre_grad_out, act_out, stats_out, hidden_ref):
    me = core[0]
    chips, _, tokens, _ = near.shape
    width = 2 * chips * 128

    def stats_of(which):
        total = jnp.zeros((tokens, 128), F32)
        squares = jnp.zeros((tokens, 128), F32)
        for chip in range(chips):
            for side in (near, far):
                value = side[chip, which].astype(F32)
                total += value
                squares += value * value
        center = jnp.sum(total, axis=1, keepdims=True) / width
        second = jnp.sum(squares, axis=1, keepdims=True) / width
        return center, lax.rsqrt(second - center * center + EPSILON)

    def chunk(which, chip):
        return both_cores(me, near[chip, which], far[chip, which])

    def cols(chip):
        return slice(chip * 256, chip * 256 + 256)

    def put(chip, rows, value):
        low, high = value[:, :128], value[:, 128:]
        own[chip, rows, :] = jnp.where(me == 0, low, high)
        other[chip, rows, :] = jnp.where(me == 0, high, low)

    center, scale = stats_of(0)
    pre = jnp.zeros((tokens, 256), F32)
    for chip in range(chips):
        normed = ((chunk(0, chip).astype(F32) - center) * scale * gain[:, cols(chip)]).astype(BF)
        pre += dot(normed, weight_a[cols(chip), :])
    act = (0.5 * pre * (1.0 + gelu_parts(pre))).astype(BF)
    for chip in range(chips):
        put(chip, slice(0, tokens), dot(act, weight_b[:, cols(chip)]).astype(BF))

    center, scale = stats_of(2)
    stats_out[...] = jnp.concatenate([jnp.broadcast_to(center, (tokens, 128)), jnp.broadcast_to(scale, (tokens, 128))], axis=1)
    pre = jnp.zeros((tokens, 256), F32)
    act_grad = jnp.zeros((tokens, 256), F32)
    for chip in range(chips):
        hidden = (chunk(2, chip).astype(F32) - center) * scale
        hidden_ref[:, cols(chip)] = hidden
        normed = (hidden * gain[:, cols(chip)]).astype(BF)
        normed_out[:, cols(chip)] = normed
        pre += dot(normed, weight_a[cols(chip), :])
        act_grad += dot(chunk(1, chip), weight_b[:, cols(chip)], ((1,), (1,)))
    tangent = gelu_parts(pre)
    act_out[...] = (0.5 * pre * (1.0 + tangent)).astype(BF)
    slope = 0.5 * (1.0 + tangent) + 0.5 * pre * (1.0 - tangent * tangent) * GELU_ROOT * (
        1.0 + 3.0 * GELU_CUBIC * pre * pre
    )
    pre_grad = (act_grad * slope).astype(BF)
    pre_grad_out[...] = pre_grad
    plain = jnp.zeros((tokens, 256), F32)
    moment = jnp.zeros((tokens, 256), F32)
    for chip in range(chips):
        term = dot(pre_grad, weight_a[cols(chip), :], ((1,), (1,))).astype(BF)
        put(chip, slice(tokens, 2 * tokens), term)
        scaled = term.astype(F32) * gain[:, cols(chip)]
        plain += scaled
        moment += scaled * hidden_ref[:, cols(chip)]
    rows = sums_to_rows(jnp.sum(plain, axis=1, keepdims=True), jnp.sum(moment, axis=1, keepdims=True))
    for chip in range(chips):
        own[chip, 2 * tokens :, :] = rows
        other[chip, 2 * tokens :, :] = rows


def pair_kernel(own, received, total):
    chips, rows, _ = own.shape
    body = rows - ROWS
    for chip in range(chips):
        total[chip, :body, :] = (own[chip, :body, :].astype(F32) + received[chip, :body, :].astype(F32)).astype(BF)
    sums = resplit(own[0, body:, :].astype(F32) + received[0, body:, :].astype(F32))
    for chip in range(chips):
        total[chip, body:, :] = sums


def finish_kernel(parts, forward_in, grad_out, fetched, stats, gain, outputs, input_grad):
    chips, rows, _ = parts.shape
    tokens = forward_in.shape[0]
    width = 2 * chips * 128
    total = jnp.zeros((rows, 128), F32)
    for chip in range(chips):
        total += parts[chip].astype(F32)
    outputs[...] = (forward_in[...].astype(F32) + total[:tokens]).astype(BF)
    scaled = total[tokens : 2 * tokens] * gain[...]
    sums = total[2 * tokens :]
    flat = jnp.concatenate([sums[:8], sums[8:]], axis=1)
    tall = jnp.concatenate([flat, jnp.zeros((120, tokens), F32)], axis=0).T
    plain_mean = (tall[:, 0:1] + tall[:, 1:2]) / width
    moment_mean = (tall[:, 2:3] + tall[:, 3:4]) / width
    center, scale = stats[:, :128], stats[:, 128:]
    hidden = (fetched[...].astype(F32) - center) * scale
    input_grad[...] = (
        grad_out[...].astype(F32) + scale * (scaled - plain_mean - hidden * moment_mean)
    ).astype(BF)


def weights_kernel(core, near, far, normed, pre_grad, act, grad_a, grad_b):
    me = core[0]
    chips = near.shape[0]
    for chip in range(chips):
        cols = slice(chip * 256, chip * 256 + 256)
        grad_a[cols, :] = dot(normed[:, cols], pre_grad[...], ((0,), (0,))).astype(BF)
        chunk = both_cores(me, near[chip, 1], far[chip, 1])
        grad_b[:, cols] = dot(act[...], chunk, ((0,), (0,))).astype(BF)


def call(kernel, out_shapes, operands, specs=None, scratch=(), flops=0, nbytes=0):
    return pl.pallas_call(
        kernel,
        out_shape=out_shapes,
        in_specs=specs or vmem(len(operands)),
        out_specs=tuple(vmem(len(out_shapes))),
        scratch_shapes=list(scratch),
        compiler_params=pltpu.CompilerParams(vmem_limit_bytes=VMEM_LIMIT),
        cost_estimate=pl.CostEstimate(flops=flops, bytes_accessed=nbytes, transcendentals=0),
    )(*operands)


def per_device(inputs, out_grads, parked_store, fetch_slot, norm_gain, weight_in, weight_out):
    forward_in = inputs[0]
    grad_out = out_grads[0]
    weight_a = weight_in[0]
    weight_b = weight_out[0]
    tokens, shard_cols = forward_in.shape
    sections, ranks = lax.axis_size("section"), lax.axis_size("tensor")
    chips = ranks // 2
    width = shard_cols * ranks
    hidden_units = weight_a.shape[1]
    rank = lax.axis_index("tensor")
    core = lax.rem(rank, 2)
    same_core = [[2 * chip + side for chip in range(chips)] for side in range(2)]
    mirror = [(s, sections - 1 - s) for s in range(sections)]
    swap = [(t, t ^ 1) for t in range(ranks)]

    returned = lax.dynamic_index_in_dim(parked_store[0], fetch_slot[0], 0, keepdims=False)
    fetched = lax.ppermute(returned, "section", mirror)
    parked = lax.ppermute(forward_in, "section", mirror)

    mine = jnp.stack([forward_in, grad_out, fetched])
    spread = jnp.broadcast_to(mine[None], (chips,) + mine.shape)
    near = lax.all_to_all(spread, "tensor", 0, 0, tiled=True, axis_index_groups=same_core)
    far = lax.ppermute(near, "tensor", swap)

    shape = jax.ShapeDtypeStruct
    part_rows = 2 * tokens + ROWS
    parts = shape((chips, part_rows, 128), BF)
    own, other, normed, pre_grad, act, stats = call(
        block_kernel,
        (
            parts,
            parts,
            shape((tokens, width), BF),
            shape((tokens, hidden_units), BF),
            shape((tokens, hidden_units), BF),
            shape((tokens, 256), F32),
        ),
        (core.reshape(1), near, far, norm_gain, weight_a, weight_b),
        specs=[pl.BlockSpec(memory_space=pltpu.SMEM)] + vmem(5),
        scratch=(pltpu.VMEM((tokens, width), F32),),
        flops=10 * tokens * width * hidden_units,
        nbytes=10 * 2**20,
    )

    received = lax.ppermute(other, "tensor", swap)
    summed = call(pair_kernel, (parts,), (own, received), nbytes=3 * 2**20)[0]
    collected = lax.all_to_all(summed, "tensor", 0, 0, tiled=True, axis_index_groups=same_core)

    gain_part = lax.dynamic_slice_in_dim(norm_gain, rank * shard_cols, shard_cols, 1)
    piece = shape((tokens, shard_cols), BF)
    outputs, input_grad = call(
        finish_kernel,
        (piece, piece),
        (collected, forward_in, grad_out, fetched, stats, gain_part),
        nbytes=2 * 2**20,
    )
    arrivals = lax.ppermute(outputs, "section", [(s, s + 1) for s in range(sections - 1)])
    sent_grads = lax.ppermute(input_grad, "section", [(s + 1, s) for s in range(sections - 1)])

    grad_a, grad_b = call(
        weights_kernel,
        (shape(weight_a.shape, BF), shape(weight_b.shape, BF)),
        (core.reshape(1), near, far, normed, pre_grad, act),
        specs=[pl.BlockSpec(memory_space=pltpu.SMEM)] + vmem(5),
        flops=4 * tokens * width * hidden_units,
        nbytes=6 * 2**20,
    )
    return (arrivals[None], sent_grads[None], parked[None], grad_a[None], grad_b[None])


def solution(mesh):
    return jax.shard_map(
        per_device,
        mesh=mesh,
        in_specs=(
            P("section", None, "tensor"),
            P("section", None, "tensor"),
            P("section", None, None, "tensor"),
            P("section"),
            P("section", None),
            P("section", None, "tensor"),
            P("section", "tensor", None),
        ),
        out_specs=(
            P("section", None, "tensor"),
            P("section", None, "tensor"),
            P("section", None, "tensor"),
            P("section", None, "tensor"),
            P("section", "tensor", None),
        ),
        check_vma=False,
    )
```

```python
import functools

import jax
import jax.numpy as jnp
from jax import lax
from jax.experimental import pallas as pl
from jax.experimental.pallas import tpu as pltpu
from jax.sharding import PartitionSpec as P

EPSILON = 1e-05
GELU_ROOT = 0.7978845608028654
GELU_CUBIC = 0.044715

BF = jnp.bfloat16
F32 = jnp.float32
ROWS = 32
VMEM_LIMIT = 16 * 2**20


def hbm(count):
    return [pl.BlockSpec(memory_space=pltpu.HBM)] * count


def vmem(count):
    return [pl.BlockSpec(memory_space=pltpu.VMEM)] * count


def dot(left, right, dims=((1,), (0,))):
    return lax.dot_general(left, right, (dims, ((), ())), preferred_element_type=F32)


def gelu_parts(values):
    inner = GELU_ROOT * (values + GELU_CUBIC * values * values * values)
    return jnp.tanh(inner)


def split_three(values):
    high = values.astype(BF)
    rest = values - high.astype(F32)
    middle = rest.astype(BF)
    return high, middle, (rest - middle.astype(F32)).astype(BF)


def columns_to_rows(columns):
    tokens = columns[0].shape[0]
    lane = lax.broadcasted_iota(jnp.int32, (tokens, 128), 1)
    wide = jnp.zeros((tokens, 128), F32)
    for index, column in enumerate(columns):
        wide = jnp.where(lane == index, column, wide)
    tall = wide.T[:8]
    return jnp.concatenate([stack_parts(tall[:, :128]), stack_parts(tall[:, 128:])], axis=0)


def stack_parts(rows):
    high, middle, low = (part.astype(F32) for part in split_three(rows[:4]))
    return jnp.concatenate([high, middle, low, jnp.zeros_like(high)], axis=0).astype(BF)


def add_parts(rows):
    halves = [rows[at : at + 4] + rows[at + 4 : at + 8] + rows[at + 8 : at + 12] for at in (0, 16)]
    return jnp.concatenate(halves, axis=1)


def both_cores(me, near, far):
    return jnp.concatenate([jnp.where(me == 0, near, far), jnp.where(me == 0, far, near)], axis=1)


def norm_stats(blocks, width):
    total, squares = 0.0, 0.0
    for block in blocks:
        value = block.astype(F32)
        total += value
        squares += value * value
    center = jnp.sum(total, axis=1, keepdims=True) / width
    second = jnp.sum(squares, axis=1, keepdims=True) / width
    return center, lax.rsqrt(second - center * center + EPSILON)


def chip_cols(chip):
    return slice(chip * 256, chip * 256 + 256)


def forward_kernel(core, near, far, gain, weight_a, weight_b, packed):
    me = core[0]
    chips, _, tokens, _ = near.shape
    hidden_units = weight_a.shape[1]
    center, scale = norm_stats([side[chip, 0] for chip in range(chips) for side in (near, far)], 256 * chips)
    pre = jnp.zeros((tokens, hidden_units), F32)
    act_grad = jnp.zeros((tokens, hidden_units), F32)
    for chip in range(chips):
        value = both_cores(me, near[chip, 0], far[chip, 0]).astype(F32)
        normed = ((value - center) * scale * gain[:, chip_cols(chip)]).astype(BF)
        pre += dot(normed, weight_a[chip_cols(chip), :])
        grad = both_cores(me, near[chip, 1], far[chip, 1])
        act_grad += dot(grad, weight_b[:, chip_cols(chip)], ((1,), (1,)))
    packed[:tokens, :hidden_units] = act_grad
    packed[:tokens, hidden_units:] = (0.5 * pre * (1.0 + gelu_parts(pre))).astype(BF).astype(F32)
    parts = [part.astype(F32) for part in split_three(gain[...])]
    gains = jnp.concatenate(parts + [jnp.zeros((13, gain.shape[1]), F32)], axis=0).astype(BF)
    gained = dot(gains, weight_a[...])
    packed[tokens:, :hidden_units] = jnp.broadcast_to(gained[0:1] + gained[1:2] + gained[2:3], (8, hidden_units))


def side_parts(side, act, pre_grad, weight_a, weight_b, parts):
    chips = parts.shape[0]
    tokens = act.shape[0]
    for chip in range(0, chips, 2):
        starts = [pl.multiple_of((chip + step) * 256 + side * 128, 128) for step in range(2)]
        columns = jnp.concatenate([weight_b[:, pl.ds(start, 128)] for start in starts], axis=1)
        branch = dot(act, columns).astype(BF)
        rows = jnp.concatenate([weight_a[pl.ds(start, 128), :] for start in starts], axis=0)
        term = dot(pre_grad, rows, ((1,), (1,))).astype(BF)
        for step in range(2):
            parts[chip + step, :tokens, :] = branch[:, step * 128 : step * 128 + 128]
            parts[chip + step, tokens : 2 * tokens, :] = term[:, step * 128 : step * 128 + 128]


def backward_kernel(core, near, far, packed, gain, weight_a, weight_b, other, normed_out, small):
    me = core[0]
    chips, tokens, _ = near.shape
    hidden_units = weight_a.shape[1]
    width = 256 * chips
    center, scale = norm_stats([side[chip] for chip in range(chips) for side in (near, far)], width)
    pre = jnp.zeros((tokens, hidden_units), F32)
    for chip in range(chips):
        hidden = (both_cores(me, near[chip], far[chip]).astype(F32) - center) * scale
        normed = (hidden * gain[:, chip_cols(chip)]).astype(BF)
        normed_out[:, chip_cols(chip)] = normed
        pre += dot(normed, weight_a[chip_cols(chip), :])
    tangent = gelu_parts(pre)
    slope = 0.5 * (1.0 + tangent) + 0.5 * pre * (1.0 - tangent * tangent) * GELU_ROOT * (
        1.0 + 3.0 * GELU_CUBIC * pre * pre
    )
    pre_grad = (packed[:tokens, :hidden_units] * slope).astype(BF)
    small[:tokens, :hidden_units] = pre_grad
    small[:tokens, hidden_units:] = (0.5 * pre * (1.0 + tangent)).astype(BF)
    wide_grad = pre_grad.astype(F32)
    plain = jnp.sum(wide_grad * packed[tokens : tokens + 1, :hidden_units], axis=1, keepdims=True)
    moment = jnp.sum(wide_grad * pre, axis=1, keepdims=True)
    share = 1.0 / (2 * chips)
    rows = columns_to_rows([plain * (1.0 / width), moment * (1.0 / width), center * share, scale * share])
    small[tokens:, :128] = rows
    for chip in range(chips):
        other[chip, 2 * tokens :, :] = rows
    side_parts(1 - me, packed[:tokens, hidden_units:].astype(BF), pre_grad, weight_a, weight_b, other)


def own_kernel(core, normed, small, packed, grad_near, grad_far, weight_a, weight_b, own, grad_a, grad_b, keep_a, keep_b, sems):
    me = core[0]
    chips, _, tokens, _ = grad_near.shape
    hidden_units = weight_a.shape[1]
    pre_grad = small[:tokens, :hidden_units]
    act = small[:tokens, hidden_units:]
    for chip in range(chips):
        cols = chip_cols(chip)
        keep_a[cols, :] = dot(normed[:, cols], pre_grad, ((0,), (0,))).astype(BF)
        grad = both_cores(me, grad_near[chip, 1], grad_far[chip, 1])
        keep_b[:, cols] = dot(act, grad, ((0,), (0,))).astype(BF)
    stores = [
        pltpu.make_async_copy(keep_a, grad_a, sems.at[0]),
        pltpu.make_async_copy(keep_b, grad_b, sems.at[1]),
    ]
    for store in stores:
        store.start()
    for chip in range(chips):
        own[chip, 2 * tokens :, :] = small[tokens:, :128]
    side_parts(me, packed[:tokens, hidden_units:].astype(BF), pre_grad, weight_a, weight_b, own)
    for store in stores:
        store.wait()


def pair_kernel(own, received, total):
    body = own.shape[1] - ROWS
    total[0, :body, :] = (own[0, :body, :].astype(F32) + received[0, :body, :].astype(F32)).astype(BF)
    sums = add_parts(own[0, body:, :].astype(F32)) + add_parts(received[0, body:, :].astype(F32))
    total[0, body:, :] = jnp.concatenate([stack_parts(sums[:, :128]), stack_parts(sums[:, 128:])], axis=0)


def chip_total(parts):
    total = parts[0].astype(F32)
    for chip in range(1, parts.shape[0]):
        total += parts[chip].astype(F32)
    return total


def finish_kernel(parts, forward_in, grad_out, fetched, gain, outputs, input_grad):
    tokens = grad_out.shape[0]
    total = chip_total(parts)
    outputs[...] = (forward_in[...].astype(F32) + total[:tokens]).astype(BF)
    scaled = total[tokens : 2 * tokens] * gain[...]
    sums = add_parts(total[2 * tokens :])
    tall = jnp.concatenate([sums, jnp.zeros((124, tokens), F32)], axis=0).T
    plain_mean, moment_mean, center, scale = (tall[:, index : index + 1] for index in range(4))
    hidden = (fetched[...].astype(F32) - center) * scale
    input_grad[...] = (
        grad_out[...].astype(F32) + scale * (scaled - plain_mean - hidden * moment_mean)
    ).astype(BF)


def store_kernel(*refs):
    count = (len(refs) - 1) // 2
    copies = [pltpu.make_async_copy(refs[i], refs[count + i], refs[-1].at[i]) for i in range(count)]
    for copy in copies:
        copy.start()
    for copy in copies:
        copy.wait()


def call(kernel, out_shapes, operands, specs=None, out_specs=None, scratch=(), grid=(), flops=0, nbytes=0):
    return pl.pallas_call(
        kernel,
        out_shape=out_shapes,
        in_specs=specs or vmem(len(operands)),
        out_specs=tuple(out_specs or vmem(len(out_shapes))),
        scratch_shapes=list(scratch),
        grid=grid,
        compiler_params=pltpu.CompilerParams(vmem_limit_bytes=VMEM_LIMIT),
        cost_estimate=pl.CostEstimate(flops=flops, bytes_accessed=nbytes, transcendentals=0),
    )(*operands)


def per_device(inputs, out_grads, parked_store, fetch_slot, norm_gain, weight_in, weight_out):
    forward_in = inputs[0]
    grad_out = out_grads[0]
    weight_a = weight_in[0]
    weight_b = weight_out[0]
    tokens, shard_cols = forward_in.shape
    sections, ranks = lax.axis_size("section"), lax.axis_size("tensor")
    chips = ranks // 2
    width = shard_cols * ranks
    hidden_units = weight_a.shape[1]
    rank = lax.axis_index("tensor")
    core = lax.rem(rank, 2)
    same_core = [[2 * chip + side for chip in range(chips)] for side in range(2)]
    mirror = [(s, sections - 1 - s) for s in range(sections)]
    swap = [(t, t ^ 1) for t in range(ranks)]

    returned = lax.dynamic_index_in_dim(parked_store[0], fetch_slot[0], 0, keepdims=False)
    fetched = lax.ppermute(returned, "section", mirror)
    parked = lax.ppermute(forward_in, "section", mirror)

    def over_chips(blocks):
        return lax.all_to_all(blocks, "tensor", 0, 0, tiled=True, axis_index_groups=same_core)

    def gather(mine):
        near = over_chips(jnp.broadcast_to(mine[None], (chips,) + mine.shape))
        return near, lax.ppermute(near, "tensor", swap)

    shape = jax.ShapeDtypeStruct
    which = core.reshape(1)
    smem = [pl.BlockSpec(memory_space=pltpu.SMEM)]

    index = lax.broadcasted_iota(jnp.int32, (chips, 2, tokens, shard_cols), 1)
    spread = jnp.where(index == 0, forward_in[None, None], grad_out[None, None])
    near = over_chips(spread)
    back_spread = jnp.broadcast_to(fetched[None], (chips,) + fetched.shape)
    near, back_spread = lax.optimization_barrier((near, back_spread))
    far = lax.ppermute(near, "tensor", swap)
    packed = call(
        forward_kernel,
        (shape((tokens + 8, 2 * hidden_units), F32),),
        (which, near, far, norm_gain, weight_a, weight_b),
        specs=smem + vmem(5),
        flops=4 * tokens * width * hidden_units,
        nbytes=4 * 2**20,
    )[0]

    back_near = over_chips(back_spread)
    back_near, packed = lax.optimization_barrier((back_near, packed))
    back_far = lax.ppermute(back_near, "tensor", swap)
    both_parts = shape((chips, 2 * tokens + ROWS, 128), BF)
    normed_shape = shape((tokens, width), BF)
    small_shape = shape((tokens + ROWS, 2 * hidden_units), BF)
    other, normed, small = call(
        backward_kernel,
        (both_parts, normed_shape, small_shape),
        (which, back_near, back_far, packed, norm_gain, weight_a, weight_b),
        specs=smem + vmem(6),
        flops=4 * tokens * width * hidden_units,
        nbytes=6 * 2**20,
    )
    received = lax.ppermute(other, "tensor", swap)
    own, grad_a, grad_b = call(
        own_kernel,
        (both_parts, shape(weight_a.shape, BF), shape(weight_b.shape, BF)),
        (which, normed, small, packed, near, far, weight_a, weight_b),
        specs=smem + vmem(7),
        out_specs=vmem(1) + hbm(2),
        scratch=(
            pltpu.VMEM(weight_a.shape, BF),
            pltpu.VMEM(weight_b.shape, BF),
            pltpu.SemaphoreType.DMA((2,)),
        ),
        flops=6 * tokens * width * hidden_units,
        nbytes=8 * 2**20,
    )

    one_chip = pl.BlockSpec((1, both_parts.shape[1], 128), lambda chip: (chip, 0, 0))
    summed = call(
        pair_kernel, (both_parts,), (own, received), specs=[one_chip] * 2, out_specs=[one_chip], grid=(chips,), nbytes=3 * 2**20
    )[0]
    collected = over_chips(summed)
    kept = lax.dynamic_index_in_dim(back_near, rank // 2, 0, keepdims=False)
    gain_part = lax.dynamic_slice_in_dim(norm_gain, rank * shard_cols, shard_cols, 1)
    piece = shape((tokens, shard_cols), BF)
    outputs, input_grad = call(
        finish_kernel,
        (piece, piece),
        (collected, forward_in, grad_out, kept, gain_part),
        nbytes=2 * 2**20,
    )
    arrivals = lax.ppermute(outputs, "section", [(s, s + 1) for s in range(sections - 1)])
    sent_grads = lax.ppermute(input_grad, "section", [(s + 1, s) for s in range(sections - 1)])

    def store(*values):
        count = len(values)
        return call(
            store_kernel,
            [shape(value.shape, value.dtype) for value in values],
            values,
            out_specs=hbm(count),
            scratch=(pltpu.SemaphoreType.DMA((count,)),),
            nbytes=count * 2**17,
        )

    parked = store(parked)[0]
    arrivals, sent_grads = store(arrivals, sent_grads)
    return (arrivals[None], sent_grads[None], parked[None], grad_a[None], grad_b[None])


def solution(mesh):
    return jax.shard_map(
        per_device,
        mesh=mesh,
        in_specs=(
            P("section", None, "tensor"),
            P("section", None, "tensor"),
            P("section", None, None, "tensor"),
            P("section"),
            P("section", None),
            P("section", None, "tensor"),
            P("section", "tensor", None),
        ),
        out_specs=(
            P("section", None, "tensor"),
            P("section", None, "tensor"),
            P("section", None, "tensor"),
            P("section", None, "tensor"),
            P("section", "tensor", None),
        ),
        check_vma=False,
    )
```

```python
import functools

import jax
import jax.numpy as jnp
from jax import lax
from jax.experimental import pallas as pl
from jax.experimental.pallas import tpu as pltpu
from jax.sharding import PartitionSpec as P

EPSILON = 1e-05
GELU_ROOT = 0.7978845608028654
GELU_CUBIC = 0.044715

BF = jnp.bfloat16
F32 = jnp.float32
ROWS = 32
VMEM_LIMIT = 16 * 2**20


def hbm(count):
    return [pl.BlockSpec(memory_space=pltpu.HBM)] * count


def vmem(count):
    return [pl.BlockSpec(memory_space=pltpu.VMEM)] * count


def dot(left, right, dims=((1,), (0,))):
    return lax.dot_general(left, right, (dims, ((), ())), preferred_element_type=F32)


def gelu_parts(values):
    inner = GELU_ROOT * (values + GELU_CUBIC * values * values * values)
    return jnp.tanh(inner)


def split_three(values):
    high = values.astype(BF)
    rest = values - high.astype(F32)
    middle = rest.astype(BF)
    return high, middle, (rest - middle.astype(F32)).astype(BF)


def columns_to_rows(columns):
    tokens = columns[0].shape[0]
    lane = lax.broadcasted_iota(jnp.int32, (tokens, 128), 1)
    wide = jnp.zeros((tokens, 128), F32)
    for index, column in enumerate(columns):
        wide = jnp.where(lane == index, column, wide)
    tall = wide.T[:8]
    return jnp.concatenate([stack_parts(tall[:, :128]), stack_parts(tall[:, 128:])], axis=0)


def stack_parts(rows):
    high, middle, low = (part.astype(F32) for part in split_three(rows[:4]))
    return jnp.concatenate([high, middle, low, jnp.zeros_like(high)], axis=0).astype(BF)


def add_parts(rows):
    halves = [rows[at : at + 4] + rows[at + 4 : at + 8] + rows[at + 8 : at + 12] for at in (0, 16)]
    return jnp.concatenate(halves, axis=1)


def both_cores(me, near, far):
    return jnp.concatenate([jnp.where(me == 0, near, far), jnp.where(me == 0, far, near)], axis=1)


def norm_stats(blocks, width):
    total, squares = 0.0, 0.0
    for block in blocks:
        value = block.astype(F32)
        total += value
        squares += value * value
    center = jnp.sum(total, axis=1, keepdims=True) / width
    second = jnp.sum(squares, axis=1, keepdims=True) / width
    return center, lax.rsqrt(second - center * center + EPSILON)


def chip_cols(chip):
    return slice(chip * 256, chip * 256 + 256)


def forward_kernel(core, near, far, gain, weight_a, weight_b, packed):
    me = core[0]
    chips, _, tokens, _ = near.shape
    hidden_units = weight_a.shape[1]
    center, scale = norm_stats([side[chip, 0] for chip in range(chips) for side in (near, far)], 256 * chips)
    pre = jnp.zeros((tokens, hidden_units), F32)
    act_grad = jnp.zeros((tokens, hidden_units), F32)
    for chip in range(chips):
        value = both_cores(me, near[chip, 0], far[chip, 0]).astype(F32)
        normed = ((value - center) * scale * gain[:, chip_cols(chip)]).astype(BF)
        pre += dot(normed, weight_a[chip_cols(chip), :])
        grad = both_cores(me, near[chip, 1], far[chip, 1])
        act_grad += dot(grad, weight_b[:, chip_cols(chip)], ((1,), (1,)))
    packed[:tokens, :hidden_units] = act_grad
    packed[:tokens, hidden_units:] = (0.5 * pre * (1.0 + gelu_parts(pre))).astype(BF).astype(F32)
    parts = [part.astype(F32) for part in split_three(gain[...])]
    gains = jnp.concatenate(parts + [jnp.zeros((13, gain.shape[1]), F32)], axis=0).astype(BF)
    gained = dot(gains, weight_a[...])
    packed[tokens:, :hidden_units] = jnp.broadcast_to(gained[0:1] + gained[1:2] + gained[2:3], (8, hidden_units))


def side_parts(side, act, pre_grad, weight_a, weight_b, parts):
    chips = parts.shape[0]
    tokens = act.shape[0]
    for chip in range(0, chips, 2):
        starts = [pl.multiple_of((chip + step) * 256 + side * 128, 128) for step in range(2)]
        columns = jnp.concatenate([weight_b[:, pl.ds(start, 128)] for start in starts], axis=1)
        branch = dot(act, columns).astype(BF)
        rows = jnp.concatenate([weight_a[pl.ds(start, 128), :] for start in starts], axis=0)
        term = dot(pre_grad, rows, ((1,), (1,))).astype(BF)
        for step in range(2):
            parts[chip + step, :tokens, :] = branch[:, step * 128 : step * 128 + 128]
            parts[chip + step, tokens : 2 * tokens, :] = term[:, step * 128 : step * 128 + 128]


def backward_kernel(core, near, far, packed, gain, weight_a, weight_b, other, normed_out, small):
    me = core[0]
    chips, tokens, _ = near.shape
    hidden_units = weight_a.shape[1]
    width = 256 * chips
    center, scale = norm_stats([side[chip] for chip in range(chips) for side in (near, far)], width)
    pre = jnp.zeros((tokens, hidden_units), F32)
    for chip in range(chips):
        hidden = (both_cores(me, near[chip], far[chip]).astype(F32) - center) * scale
        normed = (hidden * gain[:, chip_cols(chip)]).astype(BF)
        normed_out[:, chip_cols(chip)] = normed
        pre += dot(normed, weight_a[chip_cols(chip), :])
    tangent = gelu_parts(pre)
    slope = 0.5 * (1.0 + tangent) + 0.5 * pre * (1.0 - tangent * tangent) * GELU_ROOT * (
        1.0 + 3.0 * GELU_CUBIC * pre * pre
    )
    pre_grad = (packed[:tokens, :hidden_units] * slope).astype(BF)
    small[:tokens, :hidden_units] = pre_grad
    small[:tokens, hidden_units:] = (0.5 * pre * (1.0 + tangent)).astype(BF)
    wide_grad = pre_grad.astype(F32)
    plain = jnp.sum(wide_grad * packed[tokens : tokens + 1, :hidden_units], axis=1, keepdims=True)
    moment = jnp.sum(wide_grad * pre, axis=1, keepdims=True)
    share = 1.0 / (2 * chips)
    rows = columns_to_rows([plain * (1.0 / width), moment * (1.0 / width), scale * share, jnp.zeros_like(scale)])
    small[tokens:, :128] = rows
    for chip in range(chips):
        other[chip, 2 * tokens :, :] = rows
    side_parts(1 - me, packed[:tokens, hidden_units:].astype(BF), pre_grad, weight_a, weight_b, other)


def own_kernel(core, small, packed, weight_a, weight_b, own):
    tokens = small.shape[0] - ROWS
    hidden_units = weight_a.shape[1]
    for chip in range(own.shape[0]):
        own[chip, 2 * tokens :, :] = small[tokens:, :128]
    act = packed[:tokens, hidden_units:].astype(BF)
    side_parts(core[0], act, small[:tokens, :hidden_units], weight_a, weight_b, own)


def weights_kernel(core, normed, small, grad_near, grad_far, grad_a, grad_b):
    me = core[0]
    chips, _, tokens, _ = grad_near.shape
    hidden_units = grad_a.shape[1]
    pre_grad = small[:tokens, :hidden_units]
    act = small[:tokens, hidden_units:]
    for chip in range(chips):
        cols = chip_cols(chip)
        grad_a[cols, :] = dot(normed[:, cols], pre_grad, ((0,), (0,))).astype(BF)
        grad = both_cores(me, grad_near[chip, 1], grad_far[chip, 1])
        grad_b[:, cols] = dot(act, grad, ((0,), (0,))).astype(BF)


def pair_kernel(own, received, total, held, sems):
    chips, rows, _ = own.shape
    body = rows - ROWS
    sums = add_parts(own[0, body:, :].astype(F32)) + add_parts(received[0, body:, :].astype(F32))
    sums = jnp.concatenate([stack_parts(sums[:, :128]), stack_parts(sums[:, 128:])], axis=0)
    copies = []
    for chip in range(chips):
        held[chip, :body, :] = (own[chip, :body, :].astype(F32) + received[chip, :body, :].astype(F32)).astype(BF)
        held[chip, body:, :] = sums
        copies.append(pltpu.make_async_copy(held.at[chip], total.at[chip], sems.at[chip]))
        copies[-1].start()
    for copy in copies:
        copy.wait()


def chip_total(parts):
    total = parts[0].astype(F32)
    for chip in range(1, parts.shape[0]):
        total += parts[chip].astype(F32)
    return total


def finish_kernel(odd_ref, parts, forward_in, grad_out, normed, gain, inside, across):
    tokens = grad_out.shape[0]
    total = chip_total(parts)
    outputs = (forward_in[...].astype(F32) + total[:tokens]).astype(BF)
    scaled = total[tokens : 2 * tokens] * gain[...]
    sums = add_parts(total[2 * tokens :])
    tall = jnp.concatenate([sums, jnp.zeros((124, tokens), F32)], axis=0).T
    plain_mean, moment_mean, scale = (tall[:, index : index + 1] for index in range(3))
    hidden = normed[...].astype(F32) / gain[...]
    input_grad = (
        grad_out[...].astype(F32) + scale * (scaled - plain_mean - hidden * moment_mean)
    ).astype(BF)
    odd = odd_ref[0] == 1
    inside[...] = jnp.where(odd, input_grad, outputs)
    across[...] = jnp.where(odd, outputs, input_grad)


def store_kernel(*refs):
    count = (len(refs) - 1) // 2
    copies = [pltpu.make_async_copy(refs[i], refs[count + i], refs[-1].at[i]) for i in range(count)]
    for copy in copies:
        copy.start()
    for copy in copies:
        copy.wait()


def store_pair_kernel(odd_ref, across, inside, arrivals, sent_grads, sems):
    for odd in range(2):

        @pl.when(odd_ref[0] == odd)
        def _():
            copies = [
                pltpu.make_async_copy(inside, arrivals if odd else sent_grads, sems.at[0]),
                pltpu.make_async_copy(across, sent_grads if odd else arrivals, sems.at[1]),
            ]
            for copy in copies:
                copy.start()
            for copy in copies:
                copy.wait()


def call(kernel, out_shapes, operands, specs=None, out_specs=None, scratch=(), grid=(), flops=0, nbytes=0):
    return pl.pallas_call(
        kernel,
        out_shape=out_shapes,
        in_specs=specs or vmem(len(operands)),
        out_specs=tuple(out_specs or vmem(len(out_shapes))),
        scratch_shapes=list(scratch),
        grid=grid,
        compiler_params=pltpu.CompilerParams(vmem_limit_bytes=VMEM_LIMIT),
        cost_estimate=pl.CostEstimate(flops=flops, bytes_accessed=nbytes, transcendentals=0),
    )(*operands)


def per_device(inputs, out_grads, parked_store, fetch_slot, norm_gain, weight_in, weight_out):
    forward_in = inputs[0]
    grad_out = out_grads[0]
    weight_a = weight_in[0]
    weight_b = weight_out[0]
    tokens, shard_cols = forward_in.shape
    sections, ranks = lax.axis_size("section"), lax.axis_size("tensor")
    chips = ranks // 2
    width = shard_cols * ranks
    hidden_units = weight_a.shape[1]
    rank = lax.axis_index("tensor")
    core = lax.rem(rank, 2)
    same_core = [[2 * chip + side for chip in range(chips)] for side in range(2)]
    mirror = [(s, sections - 1 - s) for s in range(sections)]
    swap = [(t, t ^ 1) for t in range(ranks)]

    returned = lax.dynamic_index_in_dim(parked_store[0], fetch_slot[0], 0, keepdims=False)
    fetched = lax.ppermute(returned, "section", mirror)
    parked = lax.ppermute(forward_in, "section", mirror)

    def over_chips(blocks):
        return lax.all_to_all(blocks, "tensor", 0, 0, tiled=True, axis_index_groups=same_core)

    def gather(mine):
        near = over_chips(jnp.broadcast_to(mine[None], (chips,) + mine.shape))
        return near, lax.ppermute(near, "tensor", swap)

    shape = jax.ShapeDtypeStruct
    which = core.reshape(1)
    smem = [pl.BlockSpec(memory_space=pltpu.SMEM)]

    index = lax.broadcasted_iota(jnp.int32, (chips, 2, tokens, shard_cols), 1)
    spread = jnp.where(index == 0, forward_in[None, None], grad_out[None, None])
    near = over_chips(spread)
    back_spread = jnp.broadcast_to(fetched[None], (chips,) + fetched.shape)
    near, back_spread = lax.optimization_barrier((near, back_spread))
    far = lax.ppermute(near, "tensor", swap)
    packed = call(
        forward_kernel,
        (shape((tokens + 8, 2 * hidden_units), F32),),
        (which, near, far, norm_gain, weight_a, weight_b),
        specs=smem + vmem(5),
        flops=4 * tokens * width * hidden_units,
        nbytes=4 * 2**20,
    )[0]

    back_near = over_chips(back_spread)
    back_far = lax.ppermute(back_near, "tensor", swap)
    both_parts = shape((chips, 2 * tokens + ROWS, 128), BF)
    normed_shape = shape((tokens, width), BF)
    small_shape = shape((tokens + ROWS, 2 * hidden_units), BF)
    other, normed, small = call(
        backward_kernel,
        (both_parts, normed_shape, small_shape),
        (which, back_near, back_far, packed, norm_gain, weight_a, weight_b),
        specs=smem + vmem(6),
        flops=4 * tokens * width * hidden_units,
        nbytes=6 * 2**20,
    )
    received = lax.ppermute(other, "tensor", swap)
    own = call(
        own_kernel,
        (both_parts,),
        (which, small, packed, weight_a, weight_b),
        specs=smem + vmem(4),
        flops=2 * tokens * width * hidden_units,
        nbytes=4 * 2**20,
    )[0]
    grad_a, grad_b = call(
        weights_kernel,
        (shape(weight_a.shape, BF), shape(weight_b.shape, BF)),
        (which, normed, small, near, far),
        specs=smem + vmem(4),
        flops=4 * tokens * width * hidden_units,
        nbytes=6 * 2**20,
    )

    summed = call(
        pair_kernel,
        (both_parts,),
        (own, received),
        out_specs=hbm(1),
        scratch=(pltpu.VMEM(both_parts.shape, BF), pltpu.SemaphoreType.DMA((chips,))),
        nbytes=3 * 2**20,
    )[0]
    collected = over_chips(summed)
    collected, grad_a, grad_b = lax.optimization_barrier((collected, grad_a, grad_b))
    kept = lax.dynamic_slice_in_dim(normed, rank * shard_cols, shard_cols, 1)
    gain_part = lax.dynamic_slice_in_dim(norm_gain, rank * shard_cols, shard_cols, 1)
    piece = shape((tokens, shard_cols), BF)
    section_odd = lax.rem(lax.axis_index("section"), 2).reshape(1)
    inside, across = call(
        finish_kernel,
        (piece, piece),
        (section_odd, collected, forward_in, grad_out, kept, gain_part),
        specs=smem + vmem(5),
        nbytes=2 * 2**20,
    )
    inside = lax.ppermute(inside, "section", [(s, s ^ 1) for s in range(sections)])
    across = lax.ppermute(across, "section", [(s, s + 1 if s % 2 else s - 1) for s in range(1, sections - 1)])

    def store(*values):
        count = len(values)
        return call(
            store_kernel,
            [shape(value.shape, value.dtype) for value in values],
            values,
            out_specs=hbm(count),
            scratch=(pltpu.SemaphoreType.DMA((count,)),),
            nbytes=count * 2**17,
        )

    parked = store(parked)[0]
    arrivals, sent_grads = call(
        store_pair_kernel,
        (piece, piece),
        (section_odd, across, inside),
        specs=smem + vmem(2),
        out_specs=hbm(2),
        scratch=(pltpu.SemaphoreType.DMA((2,)),),
        nbytes=2**18,
    )
    return (arrivals[None], sent_grads[None], parked[None], grad_a[None], grad_b[None])


def solution(mesh):
    return jax.shard_map(
        per_device,
        mesh=mesh,
        in_specs=(
            P("section", None, "tensor"),
            P("section", None, "tensor"),
            P("section", None, None, "tensor"),
            P("section"),
            P("section", None),
            P("section", None, "tensor"),
            P("section", "tensor", None),
        ),
        out_specs=(
            P("section", None, "tensor"),
            P("section", None, "tensor"),
            P("section", None, "tensor"),
            P("section", None, "tensor"),
            P("section", "tensor", None),
        ),
        check_vma=False,
    )
```

```python
import functools

import jax
import jax.numpy as jnp
from jax import lax
from jax.experimental import pallas as pl
from jax.experimental.pallas import tpu as pltpu
from jax.sharding import PartitionSpec as P

EPSILON = 1e-05
GELU_ROOT = 0.7978845608028654
GELU_CUBIC = 0.044715

BF = jnp.bfloat16
F32 = jnp.float32
ROWS = 16
VMEM_LIMIT = 16 * 2**20


def hbm(count):
    return [pl.BlockSpec(memory_space=pltpu.HBM)] * count


def vmem(count):
    return [pl.BlockSpec(memory_space=pltpu.VMEM)] * count


def dot(left, right, dims=((1,), (0,))):
    return lax.dot_general(left, right, (dims, ((), ())), preferred_element_type=F32)


def gelu_parts(values):
    inner = GELU_ROOT * (values + GELU_CUBIC * values * values * values)
    return jnp.tanh(inner)


def split_three(values):
    high = values.astype(BF)
    rest = values - high.astype(F32)
    middle = rest.astype(BF)
    return high, middle, (rest - middle.astype(F32)).astype(BF)


def columns_to_rows(columns):
    lane = lax.broadcasted_iota(jnp.int32, (128, 128), 1)
    wide = jnp.zeros((128, 128), F32)
    for index, column in enumerate(columns):
        wide = jnp.where(lane == index, column, wide)
    high, middle, low = (part.astype(F32) for part in split_three(wide.T[:4]))
    return jnp.concatenate([high, middle, low, jnp.zeros_like(high)], axis=0).astype(BF)


def rows_to_columns(rows):
    sums = rows[0:4] + rows[4:8] + rows[8:12]
    tall = jnp.concatenate([sums, jnp.zeros((124, 128), F32)], axis=0).T
    return [tall[:, index : index + 1] for index in range(4)]


def norm_stats(blocks, width):
    total, squares = 0.0, 0.0
    for block in blocks:
        value = block.astype(F32)
        total += value
        squares += value * value
    center = jnp.sum(total, axis=1, keepdims=True) / width
    second = jnp.sum(squares, axis=1, keepdims=True) / width
    return center, lax.rsqrt(second - center * center + EPSILON)


def chip_cols(chip):
    return slice(chip * 256, chip * 256 + 256)


def gelu_slope(values, tangent):
    return 0.5 * (1.0 + tangent) + 0.5 * values * (1.0 - tangent * tangent) * GELU_ROOT * (
        1.0 + 3.0 * GELU_CUBIC * values * values
    )


def block_kernel(
    spent, blocks, back, gain, weight_b, weight_a, *refs
):
    del spent
    *far, parts, middle, held, normed_ref, near_a_ref, far_a_ref, far_b_ref, sems = refs
    ranks = blocks.shape[0]
    chips = ranks // 2
    tokens = back.shape[1]
    width = 128 * ranks
    units = weight_a.shape[1]
    near_load = pltpu.make_async_copy(weight_a, near_a_ref, sems.at[chips])
    loads = []
    for refs, place, axis in ((far[:-2], far_a_ref, 0), (far[-2:], far_b_ref, 1)):
        size = width // len(refs)
        for index, ref in enumerate(refs):
            part = slice(index * size, index * size + size)
            there = place.at[part, :] if axis == 0 else place.at[:, part]
            loads.append(pltpu.make_async_copy(ref, there, sems.at[chips + 1 + len(loads)]))
    near_load.start()
    for load in loads:
        load.start()
    firsts, seconds = (near_a_ref, far_a_ref), (weight_b, far_b_ref)

    def pair(ref, chip, rows):
        return jnp.concatenate([ref[2 * chip, rows, :], ref[2 * chip + 1, rows, :]], axis=1)

    def pass_of(ref, rows):
        center, scale = norm_stats([ref[rank, rows, :] for rank in range(ranks)], width)
        for chip in range(chips):
            cols = chip_cols(chip)
            normed_ref[:, cols] = ((pair(ref, chip, rows).astype(F32) - center) * scale * gain[:, cols]).astype(BF)
        return center, scale

    def put(index, side, value):
        start = (2 * index + side) * units
        middle[:tokens, start : start + units] = value.astype(BF)

    first_rows, second_rows = slice(0, tokens), slice(tokens, 2 * tokens)
    pass_of(blocks, first_rows)
    near_load.wait()
    act_grad = []
    for side in range(2):
        if side:
            for load in loads:
                load.wait()
        pre = dot(normed_ref[...], firsts[side][...])
        put(1, side, 0.5 * pre * (1.0 + gelu_parts(pre)))
        total = jnp.zeros((tokens, units), F32)
        for chip in range(chips):
            total += dot(pair(blocks, chip, second_rows), seconds[side][:, chip_cols(chip)], ((1,), (1,)))
        act_grad.append(total)
    parts_of_gain = [part.astype(F32) for part in split_three(gain[...])]
    gains = jnp.concatenate(parts_of_gain + [jnp.zeros((13, gain.shape[1]), F32)], axis=0).astype(BF)

    center, scale = pass_of(back, first_rows)
    plain, moment = 0.0, 0.0
    for side in range(2):
        pre = dot(normed_ref[...], firsts[side][...])
        tangent = gelu_parts(pre)
        pre_grad = (act_grad[side] * gelu_slope(pre, tangent)).astype(BF)
        put(0, side, pre_grad)
        put(2, side, 0.5 * pre * (1.0 + tangent))
        gained = dot(gains, firsts[side][...])
        wide = pre_grad.astype(F32)
        plain += jnp.sum(wide * (gained[0:1] + gained[1:2] + gained[2:3]), axis=1, keepdims=True)
        moment += jnp.sum(wide * pre, axis=1, keepdims=True)
    share = 1.0 / chips
    rows = columns_to_rows([plain * (1.0 / width), moment * (1.0 / width), center * share, scale * share])
    copies = []
    for chip in range(chips):
        cols = chip_cols(chip)
        branch, term = 0.0, 0.0
        for side in range(2):
            pre_grad = middle[:, side * units : side * units + units]
            act = middle[:, (2 + side) * units : (3 + side) * units]
            branch += dot(act, seconds[side][:, cols])
            term += dot(pre_grad, firsts[side][cols, :], ((1,), (1,)))
        for side in range(2):
            lanes = slice(side * 128, side * 128 + 128)
            held[2 * chip + side, :tokens, :] = branch[:, lanes].astype(BF)
            held[2 * chip + side, tokens : 2 * tokens, :] = term[:, lanes].astype(BF)
            held[2 * chip + side, 2 * tokens :, :] = rows
        both = slice(2 * chip, 2 * chip + 2)
        copies.append(pltpu.make_async_copy(held.at[both], parts.at[both], sems.at[chip]))
        copies[-1].start()
    for copy in copies:
        copy.wait()


def trade_kernel(blocks, back, middle, gain, trade, grads):
    ranks, tokens, _ = back.shape
    width = 128 * ranks
    units = middle.shape[1] // 6
    center, scale = norm_stats([back[rank] for rank in range(ranks)], width)
    for chip in range(ranks // 2):
        cols = chip_cols(chip)
        value = jnp.concatenate([back[2 * chip], back[2 * chip + 1]], axis=1).astype(F32)
        trade[:, cols] = ((value - center) * scale * gain[:, cols]).astype(BF)
        grads[:, cols] = jnp.concatenate([blocks[2 * chip + side, tokens : 2 * tokens, :] for side in range(2)], axis=1)
    trade[:, width : width + units] = middle[:, units : 2 * units]
    trade[:, width + units :] = middle[:, 5 * units :]


def weights_kernel(trade, received, middle, grads, far_grads, grad_a, grad_b, keep_a, keep_b, sems):
    width = grads.shape[1]
    units = grad_a.shape[1]
    pre_grad = jnp.concatenate([middle[:, :units], received[:, width : width + units]], axis=0)
    act = jnp.concatenate([middle[:, 4 * units : 5 * units], received[:, width + units :]], axis=0)
    stores = []
    for chip in range(width // 256):
        cols = chip_cols(chip)
        normed = jnp.concatenate([trade[:, cols], received[:, cols]], axis=0)
        keep_a[cols, :] = dot(normed, pre_grad, ((0,), (0,))).astype(BF)
        grad = jnp.concatenate([grads[:, cols], far_grads[:, cols]], axis=0)
        keep_b[:, cols] = dot(act, grad, ((0,), (0,))).astype(BF)
        stores.append(pltpu.make_async_copy(keep_a.at[cols, :], grad_a.at[cols, :], sems.at[2 * chip]))
        stores.append(pltpu.make_async_copy(keep_b.at[:, cols], grad_b.at[:, cols], sems.at[2 * chip + 1]))
        for store in stores[-2:]:
            store.start()
    for store in stores:
        store.wait()


def finish_kernel(odd_ref, parts, forward_in, grad_out, fetched, gain, inside, across):
    ranks, rows, _ = parts.shape
    tokens = (rows - ROWS) // 2
    odd = odd_ref[0] == 1
    for side in range(2):
        total = parts[side].astype(F32)
        for rank in range(2 + side, ranks, 2):
            total += parts[rank].astype(F32)
        here = slice(side * tokens, side * tokens + tokens)
        outputs = (forward_in[here, :].astype(F32) + total[:tokens]).astype(BF)
        scaled = total[tokens : 2 * tokens] * gain[...]
        plain_mean, moment_mean, center, scale = rows_to_columns(total[2 * tokens :])
        hidden = (fetched[side].astype(F32) - center) * scale
        input_grad = (
            grad_out[here, :].astype(F32) + scale * (scaled - plain_mean - hidden * moment_mean)
        ).astype(BF)
        inside[here, :] = jnp.where(odd, input_grad, outputs)
        across[here, :] = jnp.where(odd, outputs, input_grad)


def store_kernel(*refs):
    count = (len(refs) - 1) // 2
    copies = [pltpu.make_async_copy(refs[i], refs[count + i], refs[-1].at[i]) for i in range(count)]
    for copy in copies:
        copy.start()
    for copy in copies:
        copy.wait()


def store_pair_kernel(odd_ref, across, inside, arrivals, sent_grads, sems):
    for odd in range(2):

        @pl.when(odd_ref[0] == odd)
        def _():
            copies = [
                pltpu.make_async_copy(inside, arrivals if odd else sent_grads, sems.at[0]),
                pltpu.make_async_copy(across, sent_grads if odd else arrivals, sems.at[1]),
            ]
            for copy in copies:
                copy.start()
            for copy in copies:
                copy.wait()


def call(kernel, out_shapes, operands, specs=None, out_specs=None, scratch=(), aliases=None, limit=VMEM_LIMIT, flops=0, nbytes=0):
    return pl.pallas_call(
        kernel,
        out_shape=out_shapes,
        in_specs=specs or vmem(len(operands)),
        out_specs=tuple(out_specs or vmem(len(out_shapes))),
        scratch_shapes=list(scratch),
        input_output_aliases=aliases or {},
        compiler_params=pltpu.CompilerParams(vmem_limit_bytes=limit),
        cost_estimate=pl.CostEstimate(flops=flops, bytes_accessed=nbytes, transcendentals=0),
    )(*operands)


def per_device(inputs, out_grads, parked_store, fetch_slot, norm_gain, weight_in, weight_out):
    forward_in = inputs[0]
    grad_out = out_grads[0]
    weight_a = weight_in[0]
    weight_b = weight_out[0]
    tokens, shard_cols = forward_in.shape
    sections, ranks = lax.axis_size("section"), lax.axis_size("tensor")
    chips = ranks // 2
    width = shard_cols * ranks
    hidden_units = weight_a.shape[1]
    rank = lax.axis_index("tensor")
    half = tokens // 2
    mirror = [(s, sections - 1 - s) for s in range(sections)]
    swap = [(t, t ^ 1) for t in range(ranks)]

    returned = lax.dynamic_index_in_dim(parked_store[0], fetch_slot[0], 0, keepdims=False)
    fetched = lax.ppermute(returned, "section", mirror)
    parked = lax.ppermute(forward_in, "section", mirror)

    shape = jax.ShapeDtypeStruct
    smem = [pl.BlockSpec(memory_space=pltpu.SMEM)]

    def exchange(blocks):
        return lax.all_to_all(blocks, "tensor", 0, 0, tiled=True)

    pieces = (weight_a, weight_b[:, : width // 2], weight_b[:, width // 2 :])
    far = [lax.ppermute(piece, "tensor", swap) for piece in pieces]
    mine = jnp.stack([value.reshape(2, half, shard_cols) for value in (forward_in, grad_out)], axis=1)
    mine = jnp.pad(mine.reshape(2, tokens, shard_cols), ((0, 0), (0, ROWS), (0, 0)))
    spread = jnp.broadcast_to(mine[None], (chips,) + mine.shape).reshape((ranks,) + mine.shape[1:])
    blocks = exchange(spread)
    back_spread = jnp.broadcast_to(fetched.reshape(1, 2, half, shard_cols), (chips, 2, half, shard_cols))
    blocks, back_spread = lax.optimization_barrier((blocks, back_spread.reshape(ranks, half, shard_cols)))

    back = exchange(back_spread)
    parts, middle = call(
        block_kernel,
        (shape(spread.shape, BF), shape((half, 6 * hidden_units), BF)),
        (spread, blocks, back, norm_gain, weight_b, weight_a, *far),
        specs=hbm(1) + vmem(4) + hbm(1 + len(far)),
        out_specs=hbm(1) + vmem(1),
        scratch=(
            pltpu.VMEM(spread.shape, BF),
            pltpu.VMEM((half, width), BF),
            pltpu.VMEM(weight_a.shape, BF),
            pltpu.VMEM(weight_a.shape, BF),
            pltpu.VMEM(weight_b.shape, BF),
            pltpu.SemaphoreType.DMA((chips + 1 + len(far),)),
        ),
        aliases={0: 0},
        flops=10 * tokens * width * hidden_units,
        nbytes=10 * 2**20,
    )

    collected = exchange(parts)
    trade, grads = call(
        trade_kernel,
        (shape((half, width + 2 * hidden_units), BF), shape((half, width), BF)),
        (blocks, back, middle, norm_gain),
        nbytes=4 * 2**20,
    )
    grad_a, grad_b = call(
        weights_kernel,
        (shape(weight_a.shape, BF), shape(weight_b.shape, BF)),
        (trade, lax.ppermute(trade, "tensor", swap), middle, grads, lax.ppermute(grads, "tensor", swap)),
        out_specs=hbm(2),
        scratch=(
            pltpu.VMEM(weight_a.shape, BF),
            pltpu.VMEM(weight_b.shape, BF),
            pltpu.SemaphoreType.DMA((2 * chips,)),
        ),
        flops=4 * tokens * width * hidden_units,
        nbytes=6 * 2**20,
    )
    collected, grad_a, grad_b = lax.optimization_barrier((collected, grad_a, grad_b))
    gain_part = lax.dynamic_slice_in_dim(norm_gain, rank * shard_cols, shard_cols, 1)
    piece = shape((tokens, shard_cols), BF)
    kept = back_spread[:2]

    section_odd = lax.rem(lax.axis_index("section"), 2).reshape(1)
    inside, across = call(
        finish_kernel,
        (piece, piece),
        (section_odd, collected, forward_in, grad_out, kept, gain_part),
        specs=smem + vmem(5),
        nbytes=2 * 2**20,
    )
    inside = lax.ppermute(inside, "section", [(s, s ^ 1) for s in range(sections)])
    across = lax.ppermute(across, "section", [(s, s + 1 if s % 2 else s - 1) for s in range(1, sections - 1)])

    def store(*values):
        count = len(values)
        return call(
            store_kernel,
            [shape(value.shape, value.dtype) for value in values],
            values,
            out_specs=hbm(count),
            scratch=(pltpu.SemaphoreType.DMA((count,)),),
            nbytes=count * 2**17,
        )

    parked = store(parked)[0]
    arrivals, sent_grads = call(
        store_pair_kernel,
        (piece, piece),
        (section_odd, across, inside),
        specs=smem + vmem(2),
        out_specs=hbm(2),
        scratch=(pltpu.SemaphoreType.DMA((2,)),),
        nbytes=2**18,
    )
    return (arrivals[None], sent_grads[None], parked[None], grad_a[None], grad_b[None])


def solution(mesh):
    return jax.shard_map(
        per_device,
        mesh=mesh,
        in_specs=(
            P("section", None, "tensor"),
            P("section", None, "tensor"),
            P("section", None, None, "tensor"),
            P("section"),
            P("section", None),
            P("section", None, "tensor"),
            P("section", "tensor", None),
        ),
        out_specs=(
            P("section", None, "tensor"),
            P("section", None, "tensor"),
            P("section", None, "tensor"),
            P("section", None, "tensor"),
            P("section", "tensor", None),
        ),
        check_vma=False,
    )
```

```python
import functools

import jax
import jax.numpy as jnp
from jax import lax
from jax.experimental import pallas as pl
from jax.experimental.pallas import tpu as pltpu
from jax.sharding import PartitionSpec as P

EPSILON = 1e-05
GELU_ROOT = 0.7978845608028654
GELU_CUBIC = 0.044715

BF = jnp.bfloat16
F32 = jnp.float32
ROWS = 16
VMEM_LIMIT = 16 * 2**20


def hbm(count):
    return [pl.BlockSpec(memory_space=pltpu.HBM)] * count


def vmem(count):
    return [pl.BlockSpec(memory_space=pltpu.VMEM)] * count


def dot(left, right, dims=((1,), (0,))):
    return lax.dot_general(left, right, (dims, ((), ())), preferred_element_type=F32)


def gelu_parts(values):
    inner = GELU_ROOT * (values + GELU_CUBIC * values * values * values)
    return jnp.tanh(inner)


def split_three(values):
    high = values.astype(BF)
    rest = values - high.astype(F32)
    middle = rest.astype(BF)
    return high, middle, (rest - middle.astype(F32)).astype(BF)


def columns_to_rows(columns):
    lane = lax.broadcasted_iota(jnp.int32, (128, 128), 1)
    wide = jnp.zeros((128, 128), F32)
    for index, column in enumerate(columns):
        wide = jnp.where(lane == index, column, wide)
    high, middle, low = (part.astype(F32) for part in split_three(wide.T[:4]))
    return jnp.concatenate([high, middle, low, jnp.zeros_like(high)], axis=0).astype(BF)


def rows_to_columns(rows):
    sums = rows[0:4] + rows[4:8] + rows[8:12]
    tall = jnp.concatenate([sums, jnp.zeros((124, 128), F32)], axis=0).T
    return [tall[:, index : index + 1] for index in range(4)]


def norm_stats(blocks, width):
    total, squares = 0.0, 0.0
    for block in blocks:
        value = block.astype(F32)
        total += value
        squares += value * value
    center = jnp.sum(total, axis=1, keepdims=True) / width
    second = jnp.sum(squares, axis=1, keepdims=True) / width
    return center, lax.rsqrt(second - center * center + EPSILON)


def chip_cols(chip):
    return slice(chip * 256, chip * 256 + 256)


def gelu_slope(values, tangent):
    return 0.5 * (1.0 + tangent) + 0.5 * values * (1.0 - tangent * tangent) * GELU_ROOT * (
        1.0 + 3.0 * GELU_CUBIC * values * values
    )


def block_kernel(
    spent, blocks, back, gain, weight_b, weight_a, *refs
):
    del spent
    *far, parts, middle, held, normed_ref, near_a_ref, far_a_ref, far_b_ref, sems = refs
    ranks = blocks.shape[0]
    chips = ranks // 2
    tokens = back.shape[1]
    width = 128 * ranks
    units = weight_a.shape[1]
    near_load = pltpu.make_async_copy(weight_a, near_a_ref, sems.at[ranks])
    loads = []
    for refs, place, axis in ((far[:-2], far_a_ref, 0), (far[-2:], far_b_ref, 1)):
        size = width // len(refs)
        for index, ref in enumerate(refs):
            part = slice(index * size, index * size + size)
            there = place.at[part, :] if axis == 0 else place.at[:, part]
            loads.append(pltpu.make_async_copy(ref, there, sems.at[ranks + 1 + len(loads)]))
    near_load.start()
    for load in loads:
        load.start()
    firsts, seconds = (near_a_ref, far_a_ref), (weight_b, far_b_ref)

    def pair(ref, chip, rows):
        return jnp.concatenate([ref[2 * chip, rows, :], ref[2 * chip + 1, rows, :]], axis=1)

    def pass_of(ref, rows):
        center, scale = norm_stats([ref[rank, rows, :] for rank in range(ranks)], width)
        for chip in range(chips):
            cols = chip_cols(chip)
            normed_ref[:, cols] = ((pair(ref, chip, rows).astype(F32) - center) * scale * gain[:, cols]).astype(BF)
        return center, scale

    def put(index, side, value):
        start = (2 * index + side) * units
        middle[:tokens, start : start + units] = value.astype(BF)

    first_rows, second_rows = slice(0, tokens), slice(tokens, 2 * tokens)
    pass_of(blocks, first_rows)
    near_load.wait()
    act_grad = []
    for side in range(2):
        if side:
            for load in loads:
                load.wait()
        pre = dot(normed_ref[...], firsts[side][...])
        put(1, side, 0.5 * pre * (1.0 + gelu_parts(pre)))
        total = jnp.zeros((tokens, units), F32)
        for chip in range(chips):
            total += dot(pair(blocks, chip, second_rows), seconds[side][:, chip_cols(chip)], ((1,), (1,)))
        act_grad.append(total)
    parts_of_gain = [part.astype(F32) for part in split_three(gain[...])]
    gains = jnp.concatenate(parts_of_gain + [jnp.zeros((13, gain.shape[1]), F32)], axis=0).astype(BF)

    center, scale = pass_of(back, first_rows)
    plain, moment = 0.0, 0.0
    for side in range(2):
        pre = dot(normed_ref[...], firsts[side][...])
        tangent = gelu_parts(pre)
        pre_grad = (act_grad[side] * gelu_slope(pre, tangent)).astype(BF)
        put(0, side, pre_grad)
        put(2, side, 0.5 * pre * (1.0 + tangent))
        gained = dot(gains, firsts[side][...])
        wide = pre_grad.astype(F32)
        plain += jnp.sum(wide * (gained[0:1] + gained[1:2] + gained[2:3]), axis=1, keepdims=True)
        moment += jnp.sum(wide * pre, axis=1, keepdims=True)
    share = 1.0 / chips
    rows = columns_to_rows([plain * (1.0 / width), moment * (1.0 / width), center * share, scale * share])
    row = lax.broadcasted_iota(jnp.int32, rows.shape, 0)
    plain_rows = jnp.where(row == 3, share, 0.0).astype(BF)
    copies = []
    for chip in range(chips):
        cols = chip_cols(chip)
        branch, term = 0.0, 0.0
        for side in range(2):
            pre_grad = middle[:, side * units : side * units + units]
            act = middle[:, (2 + side) * units : (3 + side) * units]
            branch += dot(act, seconds[side][:, cols])
            term += dot(pre_grad, firsts[side][cols, :], ((1,), (1,)))
        for kind, value, numbers in ((0, term * gain[:, cols], rows), (1, branch, plain_rows)):
            place = kind * chips + chip
            for side in range(2):
                start = side * (tokens + ROWS)
                held[place, start : start + tokens, :] = value[:, side * 128 : side * 128 + 128].astype(BF)
                held[place, start + tokens : start + tokens + ROWS, :] = numbers
            copies.append(pltpu.make_async_copy(held.at[place], parts.at[place], sems.at[place]))
            copies[-1].start()
    for copy in copies:
        copy.wait()


def trade_kernel(blocks, back, middle, gain, trade, grads):
    ranks, tokens, _ = back.shape
    width = 128 * ranks
    units = middle.shape[1] // 6
    center, scale = norm_stats([back[rank] for rank in range(ranks)], width)
    for chip in range(ranks // 2):
        cols = chip_cols(chip)
        value = jnp.concatenate([back[2 * chip], back[2 * chip + 1]], axis=1).astype(F32)
        trade[:, cols] = ((value - center) * scale * gain[:, cols]).astype(BF)
        grads[:, cols] = jnp.concatenate([blocks[2 * chip + side, tokens : 2 * tokens, :] for side in range(2)], axis=1)
    trade[:, width : width + units] = middle[:, units : 2 * units]
    trade[:, width + units :] = middle[:, 5 * units :]


def weights_kernel(trade, received, middle, grads, far_grads, grad_a, grad_b, keep_a, keep_b, sems):
    width = grads.shape[1]
    units = grad_a.shape[1]
    pre_grad = jnp.concatenate([middle[:, :units], received[:, width : width + units]], axis=0)
    act = jnp.concatenate([middle[:, 4 * units : 5 * units], received[:, width + units :]], axis=0)
    stores = []
    for chip in range(width // 256):
        cols = chip_cols(chip)
        normed = jnp.concatenate([trade[:, cols], received[:, cols]], axis=0)
        keep_a[cols, :] = dot(normed, pre_grad, ((0,), (0,))).astype(BF)
        grad = jnp.concatenate([grads[:, cols], far_grads[:, cols]], axis=0)
        keep_b[:, cols] = dot(act, grad, ((0,), (0,))).astype(BF)
        stores.append(pltpu.make_async_copy(keep_a.at[cols, :], grad_a.at[cols, :], sems.at[2 * chip]))
        stores.append(pltpu.make_async_copy(keep_b.at[:, cols], grad_b.at[:, cols], sems.at[2 * chip + 1]))
        for store in stores[-2:]:
            store.start()
    for store in stores:
        store.wait()


def finish(parts, source, bases, values, result):
    _, ranks, rows, _ = parts.shape
    tokens = rows - ROWS
    for side in range(2):
        total = parts[source, side].astype(F32)
        for rank in range(2 + side, ranks, 2):
            total += parts[source, rank].astype(F32)
        plain_mean, moment_mean, center, scale = rows_to_columns(total[tokens:])
        hidden = (values[side].astype(F32) - center) * scale
        change = scale * (total[:tokens] - plain_mean - hidden * moment_mean)
        result[side * tokens : side * tokens + tokens, :] = (bases[side].astype(F32) + change).astype(BF)


def across_kernel(odd_ref, parts, forward_in, grad_out, fetched, across):
    odd = odd_ref[0]
    tokens = fetched.shape[1]
    halves = [slice(0, tokens), slice(tokens, 2 * tokens)]
    bases = [jnp.where(odd == 1, forward_in[here, :], grad_out[here, :]) for here in halves]
    finish(parts, odd, bases, [fetched[0], fetched[1]], across)


def inside_kernel(odd_ref, parts, paired, inside):
    tokens = inside.shape[0] // 2
    halves = [slice(0, tokens), slice(tokens, 2 * tokens)]
    finish(parts, 1 - odd_ref[0], [paired[0, here, :] for here in halves], [paired[1, here, :] for here in halves], inside)


def store_kernel(*refs):
    count = (len(refs) - 1) // 2
    copies = [pltpu.make_async_copy(refs[i], refs[count + i], refs[-1].at[i]) for i in range(count)]
    for copy in copies:
        copy.start()
    for copy in copies:
        copy.wait()


def store_pair_kernel(odd_ref, across, inside, arrivals, sent_grads, sems):
    for odd in range(2):

        @pl.when(odd_ref[0] == odd)
        def _():
            copies = [
                pltpu.make_async_copy(inside, arrivals if odd else sent_grads, sems.at[0]),
                pltpu.make_async_copy(across, sent_grads if odd else arrivals, sems.at[1]),
            ]
            for copy in copies:
                copy.start()
            for copy in copies:
                copy.wait()


def call(kernel, out_shapes, operands, specs=None, out_specs=None, scratch=(), aliases=None, limit=VMEM_LIMIT, flops=0, nbytes=0):
    return pl.pallas_call(
        kernel,
        out_shape=out_shapes,
        in_specs=specs or vmem(len(operands)),
        out_specs=tuple(out_specs or vmem(len(out_shapes))),
        scratch_shapes=list(scratch),
        input_output_aliases=aliases or {},
        compiler_params=pltpu.CompilerParams(vmem_limit_bytes=limit),
        cost_estimate=pl.CostEstimate(flops=flops, bytes_accessed=nbytes, transcendentals=0),
    )(*operands)


def per_device(inputs, out_grads, parked_store, fetch_slot, norm_gain, weight_in, weight_out):
    forward_in = inputs[0]
    grad_out = out_grads[0]
    weight_a = weight_in[0]
    weight_b = weight_out[0]
    tokens, shard_cols = forward_in.shape
    sections, ranks = lax.axis_size("section"), lax.axis_size("tensor")
    chips = ranks // 2
    width = shard_cols * ranks
    hidden_units = weight_a.shape[1]
    rank = lax.axis_index("tensor")
    half = tokens // 2
    mirror = [(s, sections - 1 - s) for s in range(sections)]
    swap = [(t, t ^ 1) for t in range(ranks)]

    returned = lax.dynamic_index_in_dim(parked_store[0], fetch_slot[0], 0, keepdims=False)
    fetched = lax.ppermute(returned, "section", mirror)
    parked = lax.ppermute(forward_in, "section", mirror)

    shape = jax.ShapeDtypeStruct
    smem = [pl.BlockSpec(memory_space=pltpu.SMEM)]

    def exchange(blocks):
        return lax.all_to_all(blocks, "tensor", 0, 0, tiled=True)

    pieces = (weight_a, weight_b[:, : width // 2], weight_b[:, width // 2 :])
    far = [lax.ppermute(piece, "tensor", swap) for piece in pieces]
    mine = jnp.stack([value.reshape(2, half, shard_cols) for value in (forward_in, grad_out)], axis=1)
    mine = jnp.pad(mine.reshape(2, tokens, shard_cols), ((0, 0), (0, 2 * ROWS), (0, 0)))
    spread = jnp.broadcast_to(mine[None], (chips,) + mine.shape).reshape((ranks,) + mine.shape[1:])
    blocks = exchange(spread)
    back_spread = jnp.broadcast_to(fetched.reshape(1, 2, half, shard_cols), (chips, 2, half, shard_cols))
    blocks, back_spread = lax.optimization_barrier((blocks, back_spread.reshape(ranks, half, shard_cols)))

    back = exchange(back_spread)
    section_odd = lax.rem(lax.axis_index("section"), 2)
    sent = jnp.stack([jnp.where(section_odd == 1, grad_out, forward_in), fetched])
    paired = lax.ppermute(sent, "section", [(s, s ^ 1) for s in range(sections)])
    back, paired = lax.optimization_barrier((back, paired))
    parts, middle = call(
        block_kernel,
        (shape(spread.shape, BF), shape((half, 6 * hidden_units), BF)),
        (spread, blocks, back, norm_gain, weight_b, weight_a, *far),
        specs=hbm(1) + vmem(4) + hbm(1 + len(far)),
        out_specs=hbm(1) + vmem(1),
        scratch=(
            pltpu.VMEM(spread.shape, BF),
            pltpu.VMEM((half, width), BF),
            pltpu.VMEM(weight_a.shape, BF),
            pltpu.VMEM(weight_a.shape, BF),
            pltpu.VMEM(weight_b.shape, BF),
            pltpu.SemaphoreType.DMA((ranks + 1 + len(far),)),
        ),
        aliases={0: 0},
        flops=10 * tokens * width * hidden_units,
        nbytes=10 * 2**20,
    )

    planes = [[section * ranks + r for section in (first, first + 1) for r in range(ranks)] for first in range(0, sections, 2)]
    block = (2, ranks, half + ROWS, shard_cols)
    collected = lax.all_to_all(
        parts.reshape((2 * ranks,) + block[2:]), ("section", "tensor"), 0, 0, tiled=True, axis_index_groups=planes
    ).reshape(block)
    trade, grads = call(
        trade_kernel,
        (shape((half, width + 2 * hidden_units), BF), shape((half, width), BF)),
        (blocks, back, middle, norm_gain),
        nbytes=4 * 2**20,
    )
    grad_a, grad_b = call(
        weights_kernel,
        (shape(weight_a.shape, BF), shape(weight_b.shape, BF)),
        (trade, lax.ppermute(trade, "tensor", swap), middle, grads, lax.ppermute(grads, "tensor", swap)),
        out_specs=hbm(2),
        scratch=(
            pltpu.VMEM(weight_a.shape, BF),
            pltpu.VMEM(weight_b.shape, BF),
            pltpu.SemaphoreType.DMA((2 * chips,)),
        ),
        flops=4 * tokens * width * hidden_units,
        nbytes=6 * 2**20,
    )
    piece = shape((tokens, shard_cols), BF)
    odd_ref = section_odd.reshape(1)
    collected, grad_a, grad_b = lax.optimization_barrier((collected, grad_a, grad_b))
    across = call(
        across_kernel,
        (piece,),
        (odd_ref, collected, forward_in, grad_out, back_spread[:2]),
        specs=smem + vmem(4),
        nbytes=2**20,
    )[0]
    across = lax.ppermute(across, "section", [(s, s + 1 if s % 2 else s - 1) for s in range(1, sections - 1)])
    inside = call(inside_kernel, (piece,), (odd_ref, collected, paired), specs=smem + vmem(2), nbytes=2**20)[0]

    def store(*values):
        count = len(values)
        return call(
            store_kernel,
            [shape(value.shape, value.dtype) for value in values],
            values,
            out_specs=hbm(count),
            scratch=(pltpu.SemaphoreType.DMA((count,)),),
            nbytes=count * 2**17,
        )

    parked = store(parked)[0]
    arrivals, sent_grads = call(
        store_pair_kernel,
        (piece, piece),
        (odd_ref, across, inside),
        specs=smem + vmem(2),
        out_specs=hbm(2),
        scratch=(pltpu.SemaphoreType.DMA((2,)),),
        nbytes=2**18,
    )
    return (arrivals[None], sent_grads[None], parked[None], grad_a[None], grad_b[None])


def solution(mesh):
    return jax.shard_map(
        per_device,
        mesh=mesh,
        in_specs=(
            P("section", None, "tensor"),
            P("section", None, "tensor"),
            P("section", None, None, "tensor"),
            P("section"),
            P("section", None),
            P("section", None, "tensor"),
            P("section", "tensor", None),
        ),
        out_specs=(
            P("section", None, "tensor"),
            P("section", None, "tensor"),
            P("section", None, "tensor"),
            P("section", None, "tensor"),
            P("section", "tensor", None),
        ),
        check_vma=False,
    )
```

```python
import functools

import jax
import jax.numpy as jnp
from jax import lax
from jax.experimental import pallas as pl
from jax.experimental.pallas import tpu as pltpu
from jax.sharding import PartitionSpec as P

EPSILON = 1e-05
GELU_ROOT = 0.7978845608028654
GELU_CUBIC = 0.044715

BF = jnp.bfloat16
F32 = jnp.float32
VMEM_LIMIT = 16 * 2**20


def hbm(count):
    return [pl.BlockSpec(memory_space=pltpu.HBM)] * count


def vmem(count):
    return [pl.BlockSpec(memory_space=pltpu.VMEM)] * count


def dot(left, right, dims=((1,), (0,))):
    return lax.dot_general(left, right, (dims, ((), ())), preferred_element_type=F32)


def gelu_parts(values):
    inner = GELU_ROOT * (values + GELU_CUBIC * values * values * values)
    return jnp.tanh(inner)


def split_three(values):
    high = values.astype(BF)
    rest = values - high.astype(F32)
    middle = rest.astype(BF)
    return high, middle, (rest - middle.astype(F32)).astype(BF)


def norm_stats(blocks, width):
    total, squares = 0.0, 0.0
    for block in blocks:
        value = block.astype(F32)
        total += value
        squares += value * value
    center = jnp.sum(total, axis=1, keepdims=True) / width
    second = jnp.sum(squares, axis=1, keepdims=True) / width
    return center, lax.rsqrt(second - center * center + EPSILON)


def chip_cols(chip):
    return slice(chip * 256, chip * 256 + 256)


def gelu_slope(values, tangent):
    return 0.5 * (1.0 + tangent) + 0.5 * values * (1.0 - tangent * tangent) * GELU_ROOT * (
        1.0 + 3.0 * GELU_CUBIC * values * values
    )


def block_kernel(
    chip_ref, spent, blocks, back, gain, weight_b, weight_a, *refs
):
    del spent
    *far, parts, middle, held, normed_ref, near_a_ref, far_a_ref, far_b_ref, sems = refs
    ranks = blocks.shape[0]
    chips = ranks // 2
    tokens = back.shape[1]
    width = 128 * ranks
    units = weight_a.shape[1]
    near_load = pltpu.make_async_copy(weight_a, near_a_ref, sems.at[ranks])
    loads = []
    for refs, place, axis in ((far[:-2], far_a_ref, 0), (far[-2:], far_b_ref, 1)):
        size = width // len(refs)
        for index, ref in enumerate(refs):
            part = slice(index * size, index * size + size)
            there = place.at[part, :] if axis == 0 else place.at[:, part]
            loads.append(pltpu.make_async_copy(ref, there, sems.at[ranks + 1 + len(loads)]))
    near_load.start()
    for load in loads:
        load.start()
    firsts, seconds = (near_a_ref, far_a_ref), (weight_b, far_b_ref)

    def pair(ref, chip, rows):
        return jnp.concatenate([ref[2 * chip, rows, :], ref[2 * chip + 1, rows, :]], axis=1)

    def pass_of(ref, rows):
        center, scale = norm_stats([ref[rank, rows, :] for rank in range(ranks)], width)
        for chip in range(chips):
            cols = chip_cols(chip)
            normed_ref[:, cols] = ((pair(ref, chip, rows).astype(F32) - center) * scale * gain[:, cols]).astype(BF)
        return center, scale

    def put(index, side, value):
        start = (2 * index + side) * units
        middle[:tokens, start : start + units] = value.astype(BF)

    first_rows, second_rows = slice(0, tokens), slice(tokens, 2 * tokens)
    pass_of(blocks, first_rows)
    near_load.wait()
    act_grad = []
    for side in range(2):
        if side:
            for load in loads:
                load.wait()
        pre = dot(normed_ref[...], firsts[side][...])
        put(1, side, 0.5 * pre * (1.0 + gelu_parts(pre)))
        total = jnp.zeros((tokens, units), F32)
        for chip in range(chips):
            total += dot(pair(blocks, chip, second_rows), seconds[side][:, chip_cols(chip)], ((1,), (1,)))
        act_grad.append(total)
    parts_of_gain = [part.astype(F32) for part in split_three(gain[...])]
    gains = jnp.concatenate(parts_of_gain + [jnp.zeros((13, gain.shape[1]), F32)], axis=0).astype(BF)

    center, scale = pass_of(back, first_rows)
    plain, moment = 0.0, 0.0
    for side in range(2):
        pre = dot(normed_ref[...], firsts[side][...])
        tangent = gelu_parts(pre)
        pre_grad = (act_grad[side] * gelu_slope(pre, tangent)).astype(BF)
        put(0, side, pre_grad)
        put(2, side, 0.5 * pre * (1.0 + tangent))
        gained = dot(gains, firsts[side][...])
        wide = pre_grad.astype(F32)
        plain += jnp.sum(wide * (gained[0:1] + gained[1:2] + gained[2:3]), axis=1, keepdims=True)
        moment += jnp.sum(wide * pre, axis=1, keepdims=True)
    plain_mean, moment_mean = plain * (1.0 / width), moment * (1.0 / width)
    copies = []
    for chip in range(chips):
        cols = chip_cols(chip)
        branch, term = 0.0, 0.0
        for side in range(2):
            pre_grad = middle[:, side * units : side * units + units]
            act = middle[:, (2 + side) * units : (3 + side) * units]
            branch += dot(act, seconds[side][:, cols])
            term += dot(pre_grad, firsts[side][cols, :], ((1,), (1,)))
        hidden = (pair(back, chip, first_rows).astype(F32) - center) * scale
        term = scale * (term * gain[:, cols] - plain_mean - hidden * moment_mean)
        mine = chip_ref[0] == chip
        term += jnp.where(mine, pair(blocks, chip, second_rows).astype(F32), 0.0)
        branch += jnp.where(mine, pair(blocks, chip, first_rows).astype(F32), 0.0)
        for kind, value in enumerate((term, branch)):
            place = kind * chips + chip
            for side in range(2):
                held[place, side * tokens : side * tokens + tokens, :] = value[:, side * 128 : side * 128 + 128].astype(BF)
            copies.append(pltpu.make_async_copy(held.at[place], parts.at[place], sems.at[place]))
            copies[-1].start()
    for copy in copies:
        copy.wait()


def trade_kernel(blocks, back, middle, gain, trade, grads):
    ranks, tokens, _ = back.shape
    width = 128 * ranks
    units = middle.shape[1] // 6
    center, scale = norm_stats([back[rank] for rank in range(ranks)], width)
    for chip in range(ranks // 2):
        cols = chip_cols(chip)
        value = jnp.concatenate([back[2 * chip], back[2 * chip + 1]], axis=1).astype(F32)
        trade[:, cols] = ((value - center) * scale * gain[:, cols]).astype(BF)
        grads[:, cols] = jnp.concatenate([blocks[2 * chip + side, tokens : 2 * tokens, :] for side in range(2)], axis=1)
    trade[:, width : width + units] = middle[:, units : 2 * units]
    trade[:, width + units :] = middle[:, 5 * units :]


def weights_kernel(trade, received, middle, grads, far_grads, grad_a, grad_b, keep_a, keep_b, sems):
    width = grads.shape[1]
    units = grad_a.shape[1]
    pre_grad = jnp.concatenate([middle[:, :units], received[:, width : width + units]], axis=0)
    act = jnp.concatenate([middle[:, 4 * units : 5 * units], received[:, width + units :]], axis=0)
    stores = []
    for chip in range(width // 256):
        cols = chip_cols(chip)
        normed = jnp.concatenate([trade[:, cols], received[:, cols]], axis=0)
        keep_a[cols, :] = dot(normed, pre_grad, ((0,), (0,))).astype(BF)
        grad = jnp.concatenate([grads[:, cols], far_grads[:, cols]], axis=0)
        keep_b[:, cols] = dot(act, grad, ((0,), (0,))).astype(BF)
        stores.append(pltpu.make_async_copy(keep_a.at[cols, :], grad_a.at[cols, :], sems.at[2 * chip]))
        stores.append(pltpu.make_async_copy(keep_b.at[:, cols], grad_b.at[:, cols], sems.at[2 * chip + 1]))
        for store in stores[-2:]:
            store.start()
    for store in stores:
        store.wait()


def finish_kernel(which, parts, result):
    _, ranks, tokens, _ = parts.shape
    for side in range(2):
        total = parts[which[0], side].astype(F32)
        for rank in range(2 + side, ranks, 2):
            total += parts[which[0], rank].astype(F32)
        result[side * tokens : side * tokens + tokens, :] = total.astype(BF)


def store_kernel(*refs):
    count = (len(refs) - 1) // 2
    copies = [pltpu.make_async_copy(refs[i], refs[count + i], refs[-1].at[i]) for i in range(count)]
    for copy in copies:
        copy.start()
    for copy in copies:
        copy.wait()


def store_pair_kernel(odd_ref, across, inside, arrivals, sent_grads, sems):
    for odd in range(2):

        @pl.when(odd_ref[0] == odd)
        def _():
            copies = [
                pltpu.make_async_copy(inside, arrivals if odd else sent_grads, sems.at[0]),
                pltpu.make_async_copy(across, sent_grads if odd else arrivals, sems.at[1]),
            ]
            for copy in copies:
                copy.start()
            for copy in copies:
                copy.wait()


def call(kernel, out_shapes, operands, specs=None, out_specs=None, scratch=(), aliases=None, limit=VMEM_LIMIT, flops=0, nbytes=0):
    return pl.pallas_call(
        kernel,
        out_shape=out_shapes,
        in_specs=specs or vmem(len(operands)),
        out_specs=tuple(out_specs or vmem(len(out_shapes))),
        scratch_shapes=list(scratch),
        input_output_aliases=aliases or {},
        compiler_params=pltpu.CompilerParams(vmem_limit_bytes=limit),
        cost_estimate=pl.CostEstimate(flops=flops, bytes_accessed=nbytes, transcendentals=0),
    )(*operands)


def per_device(inputs, out_grads, parked_store, fetch_slot, norm_gain, weight_in, weight_out):
    forward_in = inputs[0]
    grad_out = out_grads[0]
    weight_a = weight_in[0]
    weight_b = weight_out[0]
    tokens, shard_cols = forward_in.shape
    sections, ranks = lax.axis_size("section"), lax.axis_size("tensor")
    chips = ranks // 2
    width = shard_cols * ranks
    hidden_units = weight_a.shape[1]
    rank = lax.axis_index("tensor")
    half = tokens // 2
    mirror = [(s, sections - 1 - s) for s in range(sections)]
    swap = [(t, t ^ 1) for t in range(ranks)]

    returned = lax.dynamic_index_in_dim(parked_store[0], fetch_slot[0], 0, keepdims=False)
    fetched = lax.ppermute(returned, "section", mirror)
    parked = lax.ppermute(forward_in, "section", mirror)

    shape = jax.ShapeDtypeStruct
    smem = [pl.BlockSpec(memory_space=pltpu.SMEM)]

    def exchange(blocks):
        return lax.all_to_all(blocks, "tensor", 0, 0, tiled=True)

    pieces = (weight_a, weight_b[:, : width // 2], weight_b[:, width // 2 :])
    far = [lax.ppermute(piece, "tensor", swap) for piece in pieces]
    mine = jnp.stack([value.reshape(2, half, shard_cols) for value in (forward_in, grad_out)], axis=1)
    mine = mine.reshape(2, tokens, shard_cols)
    spread = jnp.broadcast_to(mine[None], (chips,) + mine.shape).reshape((ranks,) + mine.shape[1:])
    blocks = exchange(spread)
    back_spread = jnp.broadcast_to(fetched.reshape(1, 2, half, shard_cols), (chips, 2, half, shard_cols))
    blocks, back_spread = lax.optimization_barrier((blocks, back_spread.reshape(ranks, half, shard_cols)))

    back = exchange(back_spread)
    parts, middle = call(
        block_kernel,
        (shape(spread.shape, BF), shape((half, 6 * hidden_units), BF)),
        ((rank // 2).reshape(1), spread, blocks, back, norm_gain, weight_b, weight_a, *far),
        specs=smem + hbm(1) + vmem(4) + hbm(1 + len(far)),
        out_specs=hbm(1) + vmem(1),
        scratch=(
            pltpu.VMEM(spread.shape, BF),
            pltpu.VMEM((half, width), BF),
            pltpu.VMEM(weight_a.shape, BF),
            pltpu.VMEM(weight_a.shape, BF),
            pltpu.VMEM(weight_b.shape, BF),
            pltpu.SemaphoreType.DMA((ranks + 1 + len(far),)),
        ),
        aliases={1: 0},
        flops=10 * tokens * width * hidden_units,
        nbytes=10 * 2**20,
    )

    planes = [[section * ranks + r for section in (first, first + 1) for r in range(ranks)] for first in range(0, sections, 2)]
    block = (2, ranks, half, shard_cols)
    collected = lax.all_to_all(
        parts.reshape((2 * ranks,) + block[2:]), ("section", "tensor"), 0, 0, tiled=True, axis_index_groups=planes
    ).reshape(block)
    trade, grads = call(
        trade_kernel,
        (shape((half, width + 2 * hidden_units), BF), shape((half, width), BF)),
        (blocks, back, middle, norm_gain),
        nbytes=4 * 2**20,
    )
    grad_a, grad_b = call(
        weights_kernel,
        (shape(weight_a.shape, BF), shape(weight_b.shape, BF)),
        (trade, lax.ppermute(trade, "tensor", swap), middle, grads, lax.ppermute(grads, "tensor", swap)),
        out_specs=hbm(2),
        scratch=(
            pltpu.VMEM(weight_a.shape, BF),
            pltpu.VMEM(weight_b.shape, BF),
            pltpu.SemaphoreType.DMA((2 * chips,)),
        ),
        flops=4 * tokens * width * hidden_units,
        nbytes=6 * 2**20,
    )
    piece = shape((tokens, shard_cols), BF)
    odd_ref = lax.rem(lax.axis_index("section"), 2).reshape(1)
    collected, grad_a, grad_b = lax.optimization_barrier((collected, grad_a, grad_b))
    across = call(finish_kernel, (piece,), (odd_ref, collected), specs=smem + vmem(1), nbytes=2**20)[0]
    across = lax.ppermute(across, "section", [(s, s + 1 if s % 2 else s - 1) for s in range(1, sections - 1)])
    inside = call(finish_kernel, (piece,), (1 - odd_ref, collected), specs=smem + vmem(1), nbytes=2**20)[0]

    def store(*values):
        count = len(values)
        return call(
            store_kernel,
            [shape(value.shape, value.dtype) for value in values],
            values,
            out_specs=hbm(count),
            scratch=(pltpu.SemaphoreType.DMA((count,)),),
            nbytes=count * 2**17,
        )

    parked = store(parked)[0]
    arrivals, sent_grads = call(
        store_pair_kernel,
        (piece, piece),
        (odd_ref, across, inside),
        specs=smem + vmem(2),
        out_specs=hbm(2),
        scratch=(pltpu.SemaphoreType.DMA((2,)),),
        nbytes=2**18,
    )
    return (arrivals[None], sent_grads[None], parked[None], grad_a[None], grad_b[None])


def solution(mesh):
    return jax.shard_map(
        per_device,
        mesh=mesh,
        in_specs=(
            P("section", None, "tensor"),
            P("section", None, "tensor"),
            P("section", None, None, "tensor"),
            P("section"),
            P("section", None),
            P("section", None, "tensor"),
            P("section", "tensor", None),
        ),
        out_specs=(
            P("section", None, "tensor"),
            P("section", None, "tensor"),
            P("section", None, "tensor"),
            P("section", None, "tensor"),
            P("section", "tensor", None),
        ),
        check_vma=False,
    )
```

```python
import functools

import jax
import jax.numpy as jnp
from jax import lax
from jax.experimental import pallas as pl
from jax.experimental.pallas import tpu as pltpu
from jax.sharding import PartitionSpec as P

EPSILON = 1e-05
GELU_ROOT = 0.7978845608028654
GELU_CUBIC = 0.044715

BF = jnp.bfloat16
F32 = jnp.float32
VMEM_LIMIT = 16 * 2**20


def hbm(count):
    return [pl.BlockSpec(memory_space=pltpu.HBM)] * count


def vmem(count):
    return [pl.BlockSpec(memory_space=pltpu.VMEM)] * count


def dot(left, right, dims=((1,), (0,))):
    return lax.dot_general(left, right, (dims, ((), ())), preferred_element_type=F32)


def gelu_parts(values):
    inner = GELU_ROOT * (values + GELU_CUBIC * values * values * values)
    return jnp.tanh(inner)


def split_three(values):
    high = values.astype(BF)
    rest = values - high.astype(F32)
    middle = rest.astype(BF)
    return high, middle, (rest - middle.astype(F32)).astype(BF)


def norm_stats(blocks, width):
    total, squares = 0.0, 0.0
    for block in blocks:
        value = block.astype(F32)
        total += value
        squares += value * value
    center = jnp.sum(total, axis=1, keepdims=True) / width
    second = jnp.sum(squares, axis=1, keepdims=True) / width
    return center, lax.rsqrt(second - center * center + EPSILON)


def chip_cols(chip):
    return slice(chip * 256, chip * 256 + 256)


def gelu_slope(values, tangent):
    return 0.5 * (1.0 + tangent) + 0.5 * values * (1.0 - tangent * tangent) * GELU_ROOT * (
        1.0 + 3.0 * GELU_CUBIC * values * values
    )


def block_kernel(
    chip_ref, spent, blocks, back, gain, weight_b, weight_a, *refs
):
    del spent
    *far, parts, middle, held, normed_ref, near_a_ref, far_a_ref, far_b_ref, sems = refs
    ranks = blocks.shape[0]
    chips = ranks // 2
    tokens = back.shape[1]
    width = 128 * ranks
    units = weight_a.shape[1]
    near_load = pltpu.make_async_copy(weight_a, near_a_ref, sems.at[ranks])
    loads = []
    for refs, place, axis in ((far[:-2], far_a_ref, 0), (far[-2:], far_b_ref, 1)):
        size = width // len(refs)
        for index, ref in enumerate(refs):
            part = slice(index * size, index * size + size)
            there = place.at[part, :] if axis == 0 else place.at[:, part]
            loads.append(pltpu.make_async_copy(ref, there, sems.at[ranks + 1 + len(loads)]))
    near_load.start()
    for load in loads:
        load.start()
    firsts, seconds = (near_a_ref, far_a_ref), (weight_b, far_b_ref)

    def pair(ref, chip, rows):
        return jnp.concatenate([ref[2 * chip, rows, :], ref[2 * chip + 1, rows, :]], axis=1)

    def pass_of(ref, rows):
        center, scale = norm_stats([ref[rank, rows, :] for rank in range(ranks)], width)
        for chip in range(chips):
            cols = chip_cols(chip)
            normed_ref[:, cols] = ((pair(ref, chip, rows).astype(F32) - center) * scale * gain[:, cols]).astype(BF)
        return center, scale

    def put(index, side, value):
        start = (2 * index + side) * units
        middle[:tokens, start : start + units] = value.astype(BF)

    first_rows, second_rows = slice(0, tokens), slice(tokens, 2 * tokens)
    pass_of(blocks, first_rows)
    near_load.wait()
    act_grad = []
    for side in range(2):
        if side:
            for load in loads:
                load.wait()
        pre = dot(normed_ref[...], firsts[side][...])
        put(1, side, 0.5 * pre * (1.0 + gelu_parts(pre)))
        total = jnp.zeros((tokens, units), F32)
        for chip in range(chips):
            total += dot(pair(blocks, chip, second_rows), seconds[side][:, chip_cols(chip)], ((1,), (1,)))
        act_grad.append(total)
    parts_of_gain = [part.astype(F32) for part in split_three(gain[...])]
    gains = jnp.concatenate(parts_of_gain + [jnp.zeros((13, gain.shape[1]), F32)], axis=0).astype(BF)

    center, scale = pass_of(back, first_rows)
    plain, moment = 0.0, 0.0
    for side in range(2):
        pre = dot(normed_ref[...], firsts[side][...])
        tangent = gelu_parts(pre)
        pre_grad = (act_grad[side] * gelu_slope(pre, tangent)).astype(BF)
        put(0, side, pre_grad)
        put(2, side, 0.5 * pre * (1.0 + tangent))
        gained = dot(gains, firsts[side][...])
        wide = pre_grad.astype(F32)
        plain += jnp.sum(wide * (gained[0:1] + gained[1:2] + gained[2:3]), axis=1, keepdims=True)
        moment += jnp.sum(wide * pre, axis=1, keepdims=True)
    plain_mean, moment_mean = plain * (1.0 / width), moment * (1.0 / width)
    copies = []
    for chip in range(chips):
        cols = chip_cols(chip)
        branch, term = 0.0, 0.0
        for side in range(2):
            pre_grad = middle[:, side * units : side * units + units]
            act = middle[:, (2 + side) * units : (3 + side) * units]
            branch += dot(act, seconds[side][:, cols])
            term += dot(pre_grad, firsts[side][cols, :], ((1,), (1,)))
        hidden = (pair(back, chip, first_rows).astype(F32) - center) * scale
        term = scale * (term * gain[:, cols] - plain_mean - hidden * moment_mean)
        mine = chip_ref[0] == chip
        term += jnp.where(mine, pair(blocks, chip, second_rows).astype(F32), 0.0)
        branch += jnp.where(mine, pair(blocks, chip, first_rows).astype(F32), 0.0)
        for kind, value in enumerate((term, branch)):
            place = kind * chips + chip
            for side in range(2):
                held[place, side * tokens : side * tokens + tokens, :] = value[:, side * 128 : side * 128 + 128].astype(BF)
            copies.append(pltpu.make_async_copy(held.at[place], parts.at[place], sems.at[place]))
            copies[-1].start()
    for copy in copies:
        copy.wait()


def trade_kernel(back, middle, gain, trade):
    ranks, tokens, _ = back.shape
    width = 128 * ranks
    units = middle.shape[1] // 6
    center, scale = norm_stats([back[rank] for rank in range(ranks)], width)
    for chip in range(ranks // 2):
        cols = chip_cols(chip)
        value = jnp.concatenate([back[2 * chip], back[2 * chip + 1]], axis=1).astype(F32)
        trade[:, cols] = ((value - center) * scale * gain[:, cols]).astype(BF)
    trade[:, width : width + units] = middle[:, units : 2 * units]
    trade[:, width + units :] = middle[:, 5 * units :]


def grads_kernel(blocks, grads):
    ranks, rows, _ = blocks.shape
    for rank in range(ranks):
        grads[:, rank * 128 : rank * 128 + 128] = blocks[rank, rows // 2 :, :]


def weights_kernel(trade, received, middle, grads, far_grads, grad_a, grad_b, keep_a, keep_b, sems):
    width = grads.shape[1]
    units = grad_a.shape[1]
    pre_grad = jnp.concatenate([middle[:, :units], received[:, width : width + units]], axis=0)
    act = jnp.concatenate([middle[:, 4 * units : 5 * units], received[:, width + units :]], axis=0)
    stores = []
    for chip in range(width // 256):
        cols = chip_cols(chip)
        normed = jnp.concatenate([trade[:, cols], received[:, cols]], axis=0)
        keep_a[cols, :] = dot(normed, pre_grad, ((0,), (0,))).astype(BF)
        grad = jnp.concatenate([grads[:, cols], far_grads[:, cols]], axis=0)
        keep_b[:, cols] = dot(act, grad, ((0,), (0,))).astype(BF)
        stores.append(pltpu.make_async_copy(keep_a.at[cols, :], grad_a.at[cols, :], sems.at[2 * chip]))
        stores.append(pltpu.make_async_copy(keep_b.at[:, cols], grad_b.at[:, cols], sems.at[2 * chip + 1]))
        for store in stores[-2:]:
            store.start()
    for store in stores:
        store.wait()


def finish_kernel(which, parts, result):
    _, ranks, tokens, _ = parts.shape
    for side in range(2):
        total = parts[which[0], side].astype(F32)
        for rank in range(2 + side, ranks, 2):
            total += parts[which[0], rank].astype(F32)
        result[side * tokens : side * tokens + tokens, :] = total.astype(BF)


def store_kernel(*refs):
    count = (len(refs) - 1) // 2
    copies = [pltpu.make_async_copy(refs[i], refs[count + i], refs[-1].at[i]) for i in range(count)]
    for copy in copies:
        copy.start()
    for copy in copies:
        copy.wait()


def store_pair_kernel(odd_ref, across, inside, arrivals, sent_grads, sems):
    for odd in range(2):

        @pl.when(odd_ref[0] == odd)
        def _():
            copies = [
                pltpu.make_async_copy(inside, arrivals if odd else sent_grads, sems.at[0]),
                pltpu.make_async_copy(across, sent_grads if odd else arrivals, sems.at[1]),
            ]
            for copy in copies:
                copy.start()
            for copy in copies:
                copy.wait()


def call(kernel, out_shapes, operands, specs=None, out_specs=None, scratch=(), aliases=None, limit=VMEM_LIMIT, flops=0, nbytes=0):
    return pl.pallas_call(
        kernel,
        out_shape=out_shapes,
        in_specs=specs or vmem(len(operands)),
        out_specs=tuple(out_specs or vmem(len(out_shapes))),
        scratch_shapes=list(scratch),
        input_output_aliases=aliases or {},
        compiler_params=pltpu.CompilerParams(vmem_limit_bytes=limit),
        cost_estimate=pl.CostEstimate(flops=flops, bytes_accessed=nbytes, transcendentals=0),
    )(*operands)


def per_device(inputs, out_grads, parked_store, fetch_slot, norm_gain, weight_in, weight_out):
    forward_in = inputs[0]
    grad_out = out_grads[0]
    weight_a = weight_in[0]
    weight_b = weight_out[0]
    tokens, shard_cols = forward_in.shape
    sections, ranks = lax.axis_size("section"), lax.axis_size("tensor")
    chips = ranks // 2
    width = shard_cols * ranks
    hidden_units = weight_a.shape[1]
    rank = lax.axis_index("tensor")
    half = tokens // 2
    mirror = [(s, sections - 1 - s) for s in range(sections)]
    swap = [(t, t ^ 1) for t in range(ranks)]

    returned = lax.dynamic_index_in_dim(parked_store[0], fetch_slot[0], 0, keepdims=False)
    fetched = lax.ppermute(returned, "section", mirror)
    parked = lax.ppermute(forward_in, "section", mirror)

    shape = jax.ShapeDtypeStruct
    smem = [pl.BlockSpec(memory_space=pltpu.SMEM)]

    def exchange(blocks):
        return lax.all_to_all(blocks, "tensor", 0, 0, tiled=True)

    pieces = (weight_a, weight_b[:, : width // 2], weight_b[:, width // 2 :])
    far = [lax.ppermute(piece, "tensor", swap) for piece in pieces]
    mine = jnp.stack([value.reshape(2, half, shard_cols) for value in (forward_in, grad_out)], axis=1)
    mine = mine.reshape(2, tokens, shard_cols)
    spread = jnp.broadcast_to(mine[None], (chips,) + mine.shape).reshape((ranks,) + mine.shape[1:])
    blocks = exchange(spread)
    back_spread = jnp.broadcast_to(fetched.reshape(1, 2, half, shard_cols), (chips, 2, half, shard_cols))
    blocks, back_spread = lax.optimization_barrier((blocks, back_spread.reshape(ranks, half, shard_cols)))

    back = exchange(back_spread)
    parts, middle = call(
        block_kernel,
        (shape(spread.shape, BF), shape((half, 6 * hidden_units), BF)),
        ((rank // 2).reshape(1), spread, blocks, back, norm_gain, weight_b, weight_a, *far),
        specs=smem + hbm(1) + vmem(4) + hbm(1 + len(far)),
        out_specs=hbm(1) + vmem(1),
        scratch=(
            pltpu.VMEM(spread.shape, BF),
            pltpu.VMEM((half, width), BF),
            pltpu.VMEM(weight_a.shape, BF),
            pltpu.VMEM(weight_a.shape, BF),
            pltpu.VMEM(weight_b.shape, BF),
            pltpu.SemaphoreType.DMA((ranks + 1 + len(far),)),
        ),
        aliases={1: 0},
        flops=10 * tokens * width * hidden_units,
        nbytes=10 * 2**20,
    )

    planes = [[section * ranks + r for section in (first, first + 1) for r in range(ranks)] for first in range(0, sections, 2)]
    block = (2, ranks, half, shard_cols)
    collected = lax.all_to_all(
        parts.reshape((2 * ranks,) + block[2:]), ("section", "tensor"), 0, 0, tiled=True, axis_index_groups=planes
    ).reshape(block)
    trade = call(
        trade_kernel,
        (shape((half, width + 2 * hidden_units), BF),),
        (back, middle, norm_gain),
        nbytes=2 * 2**20,
    )[0]
    grads = call(grads_kernel, (shape((half, width), BF),), (blocks,), nbytes=2 * 2**20)[0]
    grad_a, grad_b = call(
        weights_kernel,
        (shape(weight_a.shape, BF), shape(weight_b.shape, BF)),
        (trade, lax.ppermute(trade, "tensor", swap), middle, grads, lax.ppermute(grads, "tensor", swap)),
        out_specs=hbm(2),
        scratch=(
            pltpu.VMEM(weight_a.shape, BF),
            pltpu.VMEM(weight_b.shape, BF),
            pltpu.SemaphoreType.DMA((2 * chips,)),
        ),
        flops=4 * tokens * width * hidden_units,
        nbytes=6 * 2**20,
    )
    piece = shape((tokens, shard_cols), BF)
    odd_ref = lax.rem(lax.axis_index("section"), 2).reshape(1)
    collected, grad_a, grad_b = lax.optimization_barrier((collected, grad_a, grad_b))
    across = call(finish_kernel, (piece,), (odd_ref, collected), specs=smem + vmem(1), nbytes=2**20)[0]
    across = lax.ppermute(across, "section", [(s, s + 1 if s % 2 else s - 1) for s in range(1, sections - 1)])
    inside = call(finish_kernel, (piece,), (1 - odd_ref, collected), specs=smem + vmem(1), nbytes=2**20)[0]

    def store(*values):
        count = len(values)
        return call(
            store_kernel,
            [shape(value.shape, value.dtype) for value in values],
            values,
            out_specs=hbm(count),
            scratch=(pltpu.SemaphoreType.DMA((count,)),),
            nbytes=count * 2**17,
        )

    parked = store(parked)[0]
    arrivals, sent_grads = call(
        store_pair_kernel,
        (piece, piece),
        (odd_ref, across, inside),
        specs=smem + vmem(2),
        out_specs=hbm(2),
        scratch=(pltpu.SemaphoreType.DMA((2,)),),
        nbytes=2**18,
    )
    return (arrivals[None], sent_grads[None], parked[None], grad_a[None], grad_b[None])


def solution(mesh):
    return jax.shard_map(
        per_device,
        mesh=mesh,
        in_specs=(
            P("section", None, "tensor"),
            P("section", None, "tensor"),
            P("section", None, None, "tensor"),
            P("section"),
            P("section", None),
            P("section", None, "tensor"),
            P("section", "tensor", None),
        ),
        out_specs=(
            P("section", None, "tensor"),
            P("section", None, "tensor"),
            P("section", None, "tensor"),
            P("section", None, "tensor"),
            P("section", "tensor", None),
        ),
        check_vma=False,
    )
```
